32 devices in a mesh: frame: 4 (over y, core), row: 8 (over z, x).
Axes of the slice: x: 2, y: 2, z: 4, core: 2. Of those that a mesh axis runs over, the one named last changes fastest.
Arguments:
- queries: bfloat16 [4, 8, 128, 1120], P('frame', 'row'), may hold values from -6 to 6
- key_proj: bfloat16 [4, 8, 128, 1120], P('frame', 'row'), may hold values from -6 to 6
- value_proj: bfloat16 [4, 8, 128, 1120], P('frame', 'row'), may hold values from -6 to 6
- attn_grad: bfloat16 [4, 8, 128, 1120], P('frame', 'row'), may hold values from -6 to 6
- conv_grad: bfloat16 [4, 8, 128, 5632], P('frame', 'row'), may hold values from -6 to 6
- conv_weight: float32 [3, 3, 5632], replicated, may hold values from -2 to 2
Outputs:
- query_grad: bfloat16 [4, 8, 128, 1120], P('frame', 'row')
- key_grad: bfloat16 [4, 8, 128, 1120], P('frame', 'row')
- value_grad: bfloat16 [4, 8, 128, 1120], P('frame', 'row')
- input_grad: bfloat16 [4, 8, 128, 5632], P('frame', 'row')
The draws below stay inside these ranges and needn't reach their ends.
All inputs are finite; a program needn't handle non-finite values.
Results may differ from the reference program's by a relative error of at most 0.001.
Values may be sent and summed in bfloat16 or wider, within the bound.
No kernel may reach another device: no remote copies, remote signals or barrier semaphores. Data moves between devices by JAX's collectives and lax.ppermute only.
A program may use at most 64 MiB of HBM per device.

```python
import math
import jax
import jax.numpy as jnp
from jax import lax

HEADS = 10
HD = 112
CH = 5632
COLS = 128
FRAMES = 4
LROWS = 8
TOKENS = 4096


def levels(stream_key, shape, shards, least, largest):
    level, own = 1.0, jax.random.fold_in(stream_key, 6)
    for axis_at, shards_of in shards:
        draws = jnp.exp(jax.random.uniform(jax.random.fold_in(own, axis_at), (shards_of,), jnp.float32, least / len(shards), largest / len(shards)))
        level = level * jnp.repeat(draws, shape[axis_at] // shards_of).reshape([-1 if axis == axis_at else 1 for axis in range(len(shape))])
    return level


def bell_draw(stream_key, dims, scale, limit, split=(), kind=jnp.bfloat16):
    values = scale * jax.random.normal(stream_key, dims, jnp.float32)
    if split:
        values = values * levels(stream_key, dims, split, -0.22, 0.18)
    return jnp.clip(values, -limit, limit).astype(kind)


def setup_inputs(seed: int = 0) -> dict:
    arg_keys = jax.random.split(jax.random.key(seed), 7)
    queries = bell_draw(arg_keys[0], (FRAMES, LROWS, COLS, HEADS * HD), 1.0, 6.0, ((0, 4), (1, 8)))
    key_proj = bell_draw(arg_keys[1], (FRAMES, LROWS, COLS, HEADS * HD), 1.0, 6.0, ((0, 4), (1, 8)))
    value_proj = bell_draw(arg_keys[2], (FRAMES, LROWS, COLS, HEADS * HD), 1.0, 6.0, ((0, 4), (1, 8)))
    attn_grad = bell_draw(arg_keys[3], (FRAMES, LROWS, COLS, HEADS * HD), 1.0, 6.0, ((0, 4), (1, 8)))
    conv_grad = bell_draw(arg_keys[4], (FRAMES, LROWS, COLS, CH), 1.0, 6.0, ((0, 4), (1, 8)))
    conv_weight = bell_draw(arg_keys[5], (3, 3, CH), 9 ** -0.5, 2.0, (), jnp.float32)
    return {"queries": queries, "key_proj": key_proj, "value_proj": value_proj, "attn_grad": attn_grad, "conv_grad": conv_grad, "conv_weight": conv_weight}


EPSILON = 1e-06
HIGH = lax.Precision.HIGHEST

def relu_feat(values):
    return jnp.maximum(values.astype(jnp.float32), jnp.float32(0.0))

def reference(queries, key_proj, value_proj, attn_grad, conv_grad, conv_weight):
    grad_scale = math.sqrt(TOKENS)

    def state_step(totals, frame_item):
        key_frame, value_frame = frame_item
        key_feat = relu_feat(key_frame).reshape(-1, HEADS, HD)
        value_rows = value_frame.astype(jnp.float32).reshape(-1, HEADS, HD)
        frame_state = jnp.einsum('nhd,nhe->hde', key_feat, value_rows, precision=HIGH)
        return ((totals[0] + frame_state, totals[1] + lax.optimization_barrier(jnp.sum(key_feat, axis=0))), None)
    start_sums = (jnp.zeros((HEADS, HD, HD), jnp.float32), jnp.zeros((HEADS, HD), jnp.float32))
    (full_state, norm_sum), _ = lax.scan(state_step, start_sums, (key_proj, value_proj))

    def weights_of(query_frame, grad_frame):
        query_feat = relu_feat(query_frame).reshape(-1, HEADS, HD)
        scaled = grad_frame.astype(jnp.float32).reshape(-1, HEADS, HD) * grad_scale
        denominator = jnp.einsum('nhd,hd->nh', query_feat, norm_sum, precision=HIGH) + EPSILON
        attn_out = jnp.einsum('nhd,hde->nhe', query_feat, full_state, precision=HIGH) / denominator[..., None]
        weighted = scaled / denominator[..., None]
        projected = lax.optimization_barrier(jnp.sum(scaled * attn_out, axis=-1)) / denominator
        return (query_feat, weighted, projected)

    def grad_step(totals, frame_item):
        query_feat, weighted, projected = weights_of(frame_item[0], frame_item[1])
        state_term = jnp.einsum('nhd,nhe->hde', query_feat, weighted, precision=HIGH)
        norm_term = jnp.einsum('nh,nhd->hd', projected, query_feat, precision=HIGH)
        return ((totals[0] + state_term, totals[1] - norm_term), None)
    (state_grad, norm_grad), _ = lax.scan(grad_step, start_sums, (queries, attn_grad))

    def finish(frame_item):
        query_frame, grad_frame, key_frame, value_frame = frame_item
        query_feat, weighted, projected = weights_of(query_frame, grad_frame)
        key_raw = key_frame.astype(jnp.float32).reshape(-1, HEADS, HD)
        value_rows = value_frame.astype(jnp.float32).reshape(-1, HEADS, HD)
        query_part = jnp.einsum('hde,nhe->nhd', full_state, weighted, precision=HIGH) - projected[..., None] * norm_sum
        key_part = jnp.einsum('hde,nhe->nhd', state_grad, value_rows, precision=HIGH) + norm_grad
        value_part = jnp.einsum('hde,nhd->nhe', state_grad, relu_feat(key_raw), precision=HIGH)
        query_part = jnp.where(query_feat > 0, query_part, jnp.float32(0.0))
        key_part = jnp.where(key_raw > 0, key_part, jnp.float32(0.0))
        frame_shape = query_frame.shape
        return (query_part.reshape(frame_shape).astype(jnp.bfloat16), key_part.reshape(frame_shape).astype(jnp.bfloat16), value_part.reshape(frame_shape).astype(jnp.bfloat16))
    query_grad, key_grad, value_grad = lax.map(finish, (queries, attn_grad, key_proj, value_proj))

    def conv_frame(grad_frame):
        grad_pad = jnp.pad(grad_frame.astype(jnp.float32), ((1, 1), (1, 1), (0, 0)))
        rows_all = grad_frame.shape[0]
        cols_all = grad_frame.shape[1]
        input_acc = jnp.zeros(grad_frame.shape, jnp.float32)
        for tap_row in range(3):
            for tap_col in range(3):
                shifted = grad_pad[2 - tap_row:2 - tap_row + rows_all, 2 - tap_col:2 - tap_col + cols_all]
                input_acc = input_acc + conv_weight[tap_row, tap_col] * shifted
        return input_acc.astype(jnp.bfloat16)
    input_grad = lax.map(conv_frame, conv_grad)
    return (query_grad, key_grad, value_grad, input_grad)
```

```python
import functools
import math

import jax
import jax.numpy as jnp
from jax import lax
from jax.experimental import pallas as pl
from jax.experimental.pallas import tpu as pltpu
from jax.sharding import Mesh, PartitionSpec as P

HEADS = 10
HD = 112
EPSILON = 1e-06
HALF = HEADS // 2
CHUNKS = 2
CHIPS = ("y", "z", "x")
F32 = jnp.float32
BF16 = jnp.bfloat16

NT = (((1,), (1,)), ((), ()))
TN = (((0,), (0,)), ((), ()))
NN = (((1,), (0,)), ((), ()))


def vmem(n):
    return [pl.BlockSpec(memory_space=pltpu.VMEM)] * n


def call(body, out_shape, args, scratch=(), flops=0):
    size = sum(math.prod(a.shape) * a.dtype.itemsize for a in list(args) + list(out_shape))
    return pl.pallas_call(
        body,
        out_shape=out_shape,
        in_specs=vmem(len(args)),
        out_specs=vmem(len(out_shape)),
        scratch_shapes=list(scratch),
        compiler_params=pltpu.CompilerParams(vmem_limit_bytes=48 * 1024 * 1024),
        cost_estimate=pl.CostEstimate(flops=flops, bytes_accessed=size, transcendentals=0),
    )(*args)


def dot(a, b, dims):
    return lax.dot_general(a, b, dims, preferred_element_type=F32)


def pieces(x):
    hi = x.astype(BF16)
    lo = (x - hi.astype(F32)).astype(BF16)
    return hi, lo


def split_heads(a_ref, b_ref, mine_ref, theirs_ref):
    core = lax.axis_index("c")
    for here in range(2):

        @pl.when(core == here)
        def _():
            for i, ref in enumerate((a_ref, b_ref)):
                for h in range(HEADS):
                    part = ref[:, h * HD : (h + 1) * HD]
                    dest = mine_ref if h // HALF == here else theirs_ref
                    dest[i, h % HALF] = part


def merge_heads(parts, n_out):
    def body(qm, qt, km, kt, q_ref, k_ref, v_ref):
        core = lax.axis_index("c")
        for here in range(2):

            @pl.when(core == here)
            def _():
                for h in range(HEADS):
                    own = h // HALF == here
                    cols = slice(h * HD, (h + 1) * HD)
                    q_ref[:, cols] = (qm if own else qt)[h % HALF]
                    k_ref[:, cols] = (km if own else kt)[0, h % HALF]
                    v_ref[:, cols] = (km if own else kt)[1, h % HALF]

    return body


def both(mine, theirs, i, h):
    return jnp.concatenate([mine[i, h], theirs[i, h]], axis=0)


def state_body(n, rows, mine, theirs, pay, whole):
    for h in range(HALF):
        key = jnp.maximum(both(mine, theirs, 0, h), 0)
        val = both(mine, theirs, 1, h)
        whole[h * HD : (h + 1) * HD] = dot(key, val, TN)
        norm = jnp.sum(key.astype(F32), axis=0, keepdims=True)
        pay[:, rows + h : rows + h + 1] = jnp.broadcast_to(norm[None], (n, 1, HD))
    for j in range(n):
        pay[j, :rows] = whole[j * rows : (j + 1) * rows]


def inverse(query, norm):
    den = jnp.sum(query * norm, axis=1, keepdims=True) + EPSILON
    return 1.0 / den


def grad_body(n, rows, scale, got, mine, theirs, pay, norm_ref, whole):
    total = got[0]
    for j in range(1, n):
        total = total + got[j]
    norm_ref[...] = total[rows : rows + HALF]
    for h in range(HALF):
        query = jnp.maximum(both(mine, theirs, 0, h), 0)
        grad = both(mine, theirs, 1, h)
        inv = inverse(query.astype(F32), total[rows + h : rows + h + 1])
        hi, lo = pieces(grad.astype(F32) * (inv * scale))
        whole[h * HD : (h + 1) * HD] = dot(query, hi, TN) + dot(query, lo, TN)
    shard = total[:rows]
    for j in range(n):
        pay[j, :rows] = shard
        pay[j, rows : 2 * rows] = whole[j * rows : (j + 1) * rows]


def query_body(n, rows, scale, tok, got, mine, theirs, norm_ref, pay, out_mine, out_theirs, whole):
    total = got[0, rows : 2 * rows]
    for j in range(1, n):
        total = total + got[j, rows : 2 * rows]
    for j in range(n):
        whole[j * rows : (j + 1) * rows] = got[j, :rows]
        pay[j, :rows] = total
    for h in range(HALF):
        query = jnp.maximum(both(mine, theirs, 0, h), 0).astype(F32)
        grad = both(mine, theirs, 1, h)
        norm = norm_ref[h : h + 1]
        inv = inverse(query, norm)
        hi, lo = pieces(whole[h * HD : (h + 1) * HD])
        prod = dot(grad, hi, NT) + dot(grad, lo, NT)
        weight = inv * scale
        proj = jnp.sum(query * prod, axis=1, keepdims=True) * weight * inv
        term = -jnp.sum(query * proj, axis=0, keepdims=True)
        pay[:, rows + h : rows + h + 1] = jnp.broadcast_to(term[None], (n, 1, HD))
        out = jnp.where(query > 0, prod * weight - proj * norm, 0.0).astype(BF16)
        out_mine[h] = out[:tok]
        out_theirs[h] = out[tok:]


def key_body(n, rows, tok, got, mine, theirs, out_mine, out_theirs, whole):
    total = got[0, rows : rows + HALF]
    for j in range(1, n):
        total = total + got[j, rows : rows + HALF]
    for j in range(n):
        whole[j * rows : (j + 1) * rows] = got[j, :rows]
    for h in range(HALF):
        key = both(mine, theirs, 0, h)
        val = both(mine, theirs, 1, h)
        hi, lo = pieces(whole[h * HD : (h + 1) * HD])
        k_out = dot(val, hi, NT) + dot(val, lo, NT) + total[h : h + 1]
        k_out = jnp.where(key > 0, k_out, 0.0).astype(BF16)
        feat = jnp.maximum(key, 0)
        v_out = (dot(feat, hi, NN) + dot(feat, lo, NN)).astype(BF16)
        out_mine[0, h] = k_out[:tok]
        out_theirs[0, h] = k_out[tok:]
        out_mine[1, h] = v_out[:tok]
        out_theirs[1, h] = v_out[tok:]


def conv_body(pair, far, weight, out):
    side = lax.axis_index("x")
    cols, width = out.shape
    even = pair[0].astype(F32)
    odd = pair[1].astype(F32)
    other = far[...].astype(F32)
    sums = []
    for j in range(3):
        w_even = weight[1 + side, pl.ds(j, 1)]
        w_odd = weight[side, pl.ds(j, 1)]
        w_other = weight[2 - 2 * side, pl.ds(j, 1)]
        sums.append(even * w_even + odd * w_odd + other * w_other)
    zero = jnp.zeros((1, width), F32)
    right = jnp.concatenate([sums[0][1:], zero], axis=0)
    left = jnp.concatenate([zero, sums[2][:-1]], axis=0)
    out[...] = (sums[1] + right + left).astype(BF16)


def conv(pair, far, weight, first, tile):
    _, cols, width = pair.shape
    return pl.pallas_call(
        conv_body,
        grid=(width // tile,),
        out_shape=jax.ShapeDtypeStruct((cols, width), BF16),
        in_specs=[
            pl.BlockSpec((2, cols, tile), lambda i: (0, 0, i)),
            pl.BlockSpec((cols, tile), lambda i: (0, i)),
            pl.BlockSpec((3, 3, tile), lambda i: (0, 0, i + first // tile)),
        ],
        out_specs=pl.BlockSpec((cols, tile), lambda i: (0, i)),
        cost_estimate=pl.CostEstimate(
            flops=20 * cols * width, bytes_accessed=8 * cols * width, transcendentals=0
        ),
    )(pair, far, weight)


def shards(queries, key_proj, value_proj, attn_grad, conv_grad, conv_weight):
    tok = queries.shape[0] * queries.shape[1] * queries.shape[2]
    tokens_all = tok * lax.axis_size(("y", "c", "z", "x"))
    scale = math.sqrt(tokens_all)
    n = lax.axis_size(CHIPS)
    rows = -(-HALF * HD // n)
    pay_one = -(-(rows + HALF) // 8) * 8
    pay_two = -(-2 * rows // 8) * 8
    swap = [(0, 1), (1, 0)]
    q, k, v, g = (a.reshape(tok, HEADS * HD) for a in (queries, key_proj, value_proj, attn_grad))
    sd = jax.ShapeDtypeStruct
    scratch = [pltpu.VMEM((n * rows, HD), F32)]
    pair_shape = [sd((2, HALF, tok, HD), BF16)] * 2

    z_size = lax.axis_size("z")
    ahead = [(2 * z, 2 * z + 2) for z in range(z_size - 1)]
    back = [(2 * z + 3, 2 * z + 1) for z in range(z_size - 1)]
    cols, ch = conv_grad.shape[2:]
    width = ch // CHUNKS
    pairs = [
        lax.all_gather(
            conv_grad.reshape(cols, ch)[:, i * width : (i + 1) * width], "x", axis=0, tiled=False
        )
        for i in range(CHUNKS)
    ]

    kv_mine, kv_send = call(split_heads, pair_shape, (k, v))
    kv_got = lax.ppermute(kv_send, "c", swap)
    qg_mine, qg_send = call(split_heads, pair_shape, (q, g))
    qg_got = lax.ppermute(qg_send, "c", swap)

    def exchange(pay):
        return lax.all_to_all(pay, CHIPS, split_axis=0, concat_axis=0, tiled=True)

    macs = HALF * 2 * tok * HD * HD
    (pay,) = call(
        functools.partial(state_body, n, rows),
        [sd((n, pay_one, HD), F32)],
        (kv_mine, kv_got),
        scratch,
        flops=2 * macs,
    )
    got = exchange(pay)
    pay, norm = call(
        functools.partial(grad_body, n, rows, scale),
        [sd((n, pay_two, HD), F32), sd((HALF, HD), F32)],
        (got, qg_mine, qg_got),
        scratch,
        flops=4 * macs,
    )
    got = exchange(pay)
    pay, query_mine, query_send = call(
        functools.partial(query_body, n, rows, scale, tok),
        [sd((n, pay_one, HD), F32)] + [sd((HALF, tok, HD), BF16)] * 2,
        (got, qg_mine, qg_got, norm),
        scratch,
        flops=4 * macs,
    )
    query_got = lax.ppermute(query_send, "c", swap)
    got = exchange(pay)
    key_mine, key_send = call(
        functools.partial(key_body, n, rows, tok),
        pair_shape,
        (got, kv_mine, kv_got),
        scratch,
        flops=8 * macs,
    )
    key_got = lax.ppermute(key_send, "c", swap)
    outs = call(
        merge_heads(None, 3),
        [sd((tok, HEADS * HD), BF16)] * 3,
        (query_mine, query_got, key_mine, key_got),
    )

    side = lax.axis_index("x")
    made = []
    for i, pair in enumerate(pairs):
        near = lax.dynamic_index_in_dim(pair, 1 - side, axis=0, keepdims=False)
        far = lax.ppermute(near, ("z", "x"), ahead + back)
        made.append(conv(pair, far, conv_weight, i * width, 256))
    input_grad = jnp.concatenate(made, axis=1)
    return tuple(o.reshape(queries.shape) for o in outs) + (input_grad.reshape(conv_grad.shape),)


def solution(mesh):
    frames, bands = mesh.shape["frame"], mesh.shape["row"]
    fine = Mesh(mesh.devices.reshape(frames // 2, 2, bands // 2, 2), ("y", "c", "z", "x"))
    split = P(("y", "c"), ("z", "x"), None, None)
    return jax.shard_map(
        shards,
        mesh=fine,
        in_specs=(split,) * 5 + (P(),),
        out_specs=(split,) * 4,
        check_vma=False,
    )
```

```python
import functools
import math

import jax
import jax.numpy as jnp
from jax import lax
from jax.experimental import pallas as pl
from jax.experimental.pallas import tpu as pltpu
from jax.sharding import Mesh, PartitionSpec as P

HEADS = 10
HD = 112
EPSILON = 1e-06
HALF = HEADS // 2
LANES = 128
CHIPS = ("y", "z", "x")
F32 = jnp.float32
BF16 = jnp.bfloat16

NT = (((1,), (1,)), ((), ()))
TN = (((0,), (0,)), ((), ()))
NN = (((1,), (0,)), ((), ()))


def vmem(n):
    return [pl.BlockSpec(memory_space=pltpu.VMEM)] * n


def call(body, out_shape, args, scratch=(), flops=0):
    size = sum(math.prod(a.shape) * a.dtype.itemsize for a in list(args) + list(out_shape))
    return pl.pallas_call(
        body,
        out_shape=out_shape,
        in_specs=vmem(len(args)),
        out_specs=vmem(len(out_shape)),
        scratch_shapes=list(scratch),
        compiler_params=pltpu.CompilerParams(vmem_limit_bytes=48 * 1024 * 1024),
        cost_estimate=pl.CostEstimate(flops=flops, bytes_accessed=size, transcendentals=0),
    )(*args)


def dot(a, b, dims):
    return lax.dot_general(a, b, dims, preferred_element_type=F32)


def pieces(x):
    hi = x.astype(BF16)
    lo = (x - hi.astype(F32)).astype(BF16)
    return hi, lo


def pieces3(x):
    hi = x.astype(BF16)
    mid, lo = pieces(x - hi.astype(F32))
    return [hi, mid, lo]


def exact_rows(row, mat, dims):
    stack = jnp.concatenate(pieces3(row), axis=0)
    return jnp.sum(dot(stack, mat, dims), axis=0, keepdims=True)


def send_half(a_ref, b_ref, send_ref):
    there = 1 - lax.axis_index("c")
    size = send_ref.shape[1]
    part = pl.ds(pl.multiple_of(there * size, 16), size)
    send_ref[0] = a_ref[part]
    send_ref[1] = b_ref[part]


def merge_half(qm, qt, km, kt, q_ref, k_ref, v_ref):
    core = lax.axis_index("c")
    size = qm.shape[0]
    mine = pl.ds(pl.multiple_of(core * size, 16), size)
    theirs = pl.ds(pl.multiple_of((1 - core) * size, 16), size)
    q_ref[mine] = qm[...]
    q_ref[theirs] = qt[...]
    k_ref[mine] = km[0]
    k_ref[theirs] = kt[0]
    v_ref[mine] = km[1]
    v_ref[theirs] = kt[1]


def head_of(ref, got, i, h):
    start = lax.axis_index("c") * (HALF * HD) + h * HD
    own = ref[pl.ds(pl.multiple_of(start, 16), HD)]
    return jnp.concatenate([own, got[i, h * HD : (h + 1) * HD]], axis=1)


def columns(rows):
    wide = jnp.concatenate([rows, jnp.zeros((HALF, LANES - HD), F32)], axis=1)
    tall = jnp.concatenate([wide, jnp.zeros((8 - HALF, LANES), F32)], axis=0)
    return jnp.transpose(tall)


def spread(row, n):
    return jnp.broadcast_to(row[None], (n, 1, HD))


def sum_of(got, n, first, last):
    total = got[0, first:last]
    for j in range(1, n):
        total = total + got[j, first:last]
    return total


def state_body(n, rows, k_ref, v_ref, kv_got, pay, whole):
    for h in range(HALF):
        key = jnp.maximum(head_of(k_ref, kv_got, 0, h), 0)
        val = head_of(v_ref, kv_got, 1, h)
        whole[h * HD : (h + 1) * HD] = dot(key, val, NT)
        norm = dot(jnp.ones((8, key.shape[1]), BF16), key, NT)[:1]
        pay[:, rows + h : rows + h + 1] = spread(norm, n)
    for j in range(n):
        pay[j, :rows] = whole[j * rows : (j + 1) * rows]


def grad_body(n, rows, scale, got, q_ref, g_ref, qg_got, pay, norm_ref, inv_ref, whole):
    total = sum_of(got, n, 0, rows + HALF)
    norm_ref[...] = total[rows:]
    for h in range(HALF):
        query = jnp.maximum(head_of(q_ref, qg_got, 0, h), 0)
        grad = head_of(g_ref, qg_got, 1, h)
        inv = 1.0 / (exact_rows(total[rows + h : rows + h + 1], query, NN) + EPSILON)
        inv_ref[h : h + 1] = inv
        hi, lo = pieces(grad.astype(F32) * (inv * scale))
        whole[h * HD : (h + 1) * HD] = dot(query, hi, NT) + dot(query, lo, NT)
    shard = total[:rows]
    for j in range(n):
        pay[j, :rows] = shard
        pay[j, rows : 2 * rows] = whole[j * rows : (j + 1) * rows]


def query_body(
    n, rows, scale, got, q_ref, g_ref, qg_got, norm_ref, inv_ref, pay, out_mine, out_theirs, whole
):
    total = sum_of(got, n, rows, 2 * rows)
    for j in range(n):
        whole[j * rows : (j + 1) * rows] = got[j, :rows]
        pay[j, :rows] = total
    norms = columns(norm_ref[...])
    tok = out_mine.shape[1]
    for h in range(HALF):
        part = slice(h * HD, (h + 1) * HD)
        feat = jnp.maximum(head_of(q_ref, qg_got, 0, h), 0)
        query = feat.astype(F32)
        grad = head_of(g_ref, qg_got, 1, h)
        hi, lo = pieces(whole[part])
        prod = dot(hi, grad, NN) + dot(lo, grad, NN)
        inv = inv_ref[h : h + 1]
        weight = inv * scale
        proj = jnp.sum(query * prod, axis=0, keepdims=True) * weight * inv
        pay[:, rows + h : rows + h + 1] = spread(-exact_rows(proj, feat, NT), n)
        out = prod * weight - norms[:HD, h : h + 1] * proj
        out = jnp.where(query > 0, out, 0.0).astype(BF16)
        out_mine[part] = out[:, :tok]
        out_theirs[part] = out[:, tok:]


def key_body(n, rows, got, k_ref, v_ref, kv_got, out_mine, out_theirs, whole):
    for j in range(n):
        whole[j * rows : (j + 1) * rows] = got[j, :rows]
    norms = columns(sum_of(got, n, rows, rows + HALF))
    tok = out_mine.shape[2]
    for h in range(HALF):
        part = slice(h * HD, (h + 1) * HD)
        key = head_of(k_ref, kv_got, 0, h)
        val = head_of(v_ref, kv_got, 1, h)
        hi, lo = pieces(whole[part])
        k_out = dot(hi, val, NN) + dot(lo, val, NN) + norms[:HD, h : h + 1]
        k_out = jnp.where(key.astype(F32) > 0, k_out, 0.0).astype(BF16)
        feat = jnp.maximum(key, 0)
        v_out = (dot(hi, feat, TN) + dot(lo, feat, TN)).astype(BF16)
        out_mine[0, part] = k_out[:, :tok]
        out_theirs[0, part] = k_out[:, tok:]
        out_mine[1, part] = v_out[:, :tok]
        out_theirs[1, part] = v_out[:, tok:]


def shift(x, step):
    rows = lax.broadcasted_iota(jnp.int32, x.shape, 0)
    moved = pltpu.roll(x, step % x.shape[0], 0)
    edge = 0 if step > 0 else x.shape[0] - 1
    return jnp.where(rows == edge, 0.0, moved)


def taps(sources, weight, picks, lanes):
    planes = [ref[:, lanes].astype(F32) for ref in sources]

    def column(j):
        return sum(p * weight[i, pl.ds(j, 1), lanes] for p, i in zip(planes, picks))

    return (column(1) + shift(column(0), -1) + shift(column(2), 1)).astype(BF16)


def halve_body(row, mine, send):
    side = lax.axis_index("x")
    width = mine.shape[1]
    for here in range(2):

        @pl.when(side == here)
        def _():
            mine[...] = row[0, 0, :, here * width : (here + 1) * width]
            send[...] = row[0, 0, :, (1 - here) * width : (2 - here) * width]


def send_body(mine, got, far, weight, out):
    side = lax.axis_index("x")
    width = mine.shape[1]

    @pl.loop(0, width // LANES)
    def _(t):
        lanes = pl.ds(pl.multiple_of(t * LANES, LANES), LANES)
        out[:, lanes] = taps((got, mine, far), weight, (1, 2 - 2 * side, 2 * side), lanes)


def keep_body(mine, got, far, back, weight, out):
    side = lax.axis_index("x")
    width = mine.shape[1]

    @pl.loop(0, width // LANES)
    def _(t):
        at = t * LANES
        lanes = pl.ds(pl.multiple_of(at, LANES), LANES)
        here = pl.ds(pl.multiple_of(side * width + at, LANES), LANES)
        there = pl.ds(pl.multiple_of((1 - side) * width + at, LANES), LANES)
        out[0, 0, :, here] = taps((mine, got, far), weight, (1, 2 * side, 2 - 2 * side), lanes)
        out[0, 0, :, there] = back[:, lanes]


def shards(queries, key_proj, value_proj, attn_grad, conv_grad, conv_weight):
    tok = queries.shape[0] * queries.shape[1] * queries.shape[2]
    tokens_all = tok * lax.axis_size(("y", "c", "z", "x"))
    scale = math.sqrt(tokens_all)
    n = lax.axis_size(CHIPS)
    rows = -(-HALF * HD // n)
    pay_one = -(-(rows + HALF) // 8) * 8
    pay_two = -(-2 * rows // 8) * 8
    swap = [(0, 1), (1, 0)]
    sd = jax.ShapeDtypeStruct
    scratch = [pltpu.VMEM((n * rows, HD), F32)]
    half = HALF * HD
    pair_shape = sd((2, half, tok), BF16)
    q, k, v, g = (
        jnp.swapaxes(a, 2, 3).reshape(2 * half, tok)
        for a in (queries, key_proj, value_proj, attn_grad)
    )

    z_size = lax.axis_size("z")
    ahead = [(z, z + 1) for z in range(z_size - 1)]
    even_up = [(2 * i, 2 * j) for i, j in ahead]
    even_down = [(2 * j, 2 * i) for i, j in ahead]
    odd_up = [(2 * i + 1, 2 * j + 1) for i, j in ahead]
    odd_down = [(2 * j + 1, 2 * i + 1) for i, j in ahead]
    cols, ch = conv_grad.shape[2:]
    width = ch // 2
    half_shape = sd((cols, width), BF16)
    row_mine, row_send = call(halve_body, [half_shape] * 2, (conv_grad,))
    row_got = lax.ppermute(row_send, "x", swap)
    far_own = lax.ppermute(row_mine, ("z", "x"), even_down + odd_up)
    far_fwd = lax.ppermute(row_got, ("z", "x"), even_up + odd_down)
    side = lax.axis_index("x")
    weight = lax.dynamic_slice_in_dim(conv_weight, side * width, width, axis=2)
    (out_send,) = call(
        send_body, [half_shape], (row_mine, row_got, far_own, weight), flops=20 * cols * width
    )
    out_got = lax.ppermute(out_send, "x", swap)
    (input_grad,) = call(
        keep_body,
        [sd(conv_grad.shape, BF16)],
        (row_mine, row_got, far_fwd, out_got, weight),
        flops=20 * cols * width,
    )

    kv_send = call(send_half, [pair_shape], (k, v))[0]
    kv_got = lax.ppermute(kv_send, "c", swap)
    qg_send = call(send_half, [pair_shape], (q, g))[0]
    qg_got = lax.ppermute(qg_send, "c", swap)

    def exchange(pay):
        return lax.all_to_all(pay, CHIPS, split_axis=0, concat_axis=0, tiled=True)

    macs = HALF * 2 * tok * HD * HD
    (pay,) = call(
        functools.partial(state_body, n, rows),
        [sd((n, pay_one, HD), F32)],
        (k, v, kv_got),
        scratch,
        flops=2 * macs,
    )
    got = exchange(pay)
    pay, norm, inv = call(
        functools.partial(grad_body, n, rows, scale),
        [sd((n, pay_two, HD), F32), sd((HALF, HD), F32), sd((HALF, 2 * tok), F32)],
        (got, q, g, qg_got),
        scratch,
        flops=4 * macs,
    )
    got = exchange(pay)
    pay, query_mine, query_send = call(
        functools.partial(query_body, n, rows, scale),
        [sd((n, pay_one, HD), F32)] + [sd((half, tok), BF16)] * 2,
        (got, q, g, qg_got, norm, inv),
        scratch,
        flops=4 * macs,
    )
    query_got = lax.ppermute(query_send, "c", swap)
    got = exchange(pay)
    key_mine, key_send = call(
        functools.partial(key_body, n, rows),
        [pair_shape] * 2,
        (got, k, v, kv_got),
        scratch,
        flops=8 * macs,
    )
    key_got = lax.ppermute(key_send, "c", swap)
    outs = call(
        merge_half,
        [sd((2 * half, tok), BF16)] * 3,
        (query_mine, query_got, key_mine, key_got),
    )
    outs = [jnp.swapaxes(o.reshape(*queries.shape[:2], 2 * half, -1), 2, 3) for o in outs]
    return (*outs, input_grad)


def solution(mesh):
    frames, bands = mesh.shape["frame"], mesh.shape["row"]
    fine = Mesh(mesh.devices.reshape(frames // 2, 2, bands // 2, 2), ("y", "c", "z", "x"))
    split = P(("y", "c"), ("z", "x"), None, None)
    return jax.shard_map(
        shards,
        mesh=fine,
        in_specs=(split,) * 5 + (P(),),
        out_specs=(split,) * 4,
        check_vma=False,
    )
```

```python
import functools
import math

import jax
import jax.numpy as jnp
from jax import lax
from jax.experimental import pallas as pl
from jax.experimental.pallas import tpu as pltpu
from jax.sharding import Mesh, PartitionSpec as P

HEADS = 10
HD = 112
EPSILON = 1e-06
HALF = HEADS // 2
LANES = 128
CHIPS = ("y", "z", "x")
F32 = jnp.float32
BF16 = jnp.bfloat16

NT = (((1,), (1,)), ((), ()))
TN = (((0,), (0,)), ((), ()))
NN = (((1,), (0,)), ((), ()))


def held_in_hbm(x):
    return pltpu.with_memory_space_constraint(x, pltpu.HBM)


def call(body, outs, args, scratch=(), flops=0, after=(), hbm_in=False, hbm_out=False, pinned=False):
    size = sum(math.prod(a.shape) * a.dtype.itemsize for a in list(args) + list(outs))
    fast = pl.BlockSpec(memory_space=pltpu.VMEM)
    slow = pl.BlockSpec(memory_space=pltpu.HBM)
    scratch = list(scratch)
    if pinned:
        scratch += [pltpu.VMEM(outs[0].shape, outs[0].dtype), pltpu.SemaphoreType.DMA((1,))]

    def ordered(*refs):
        ins = refs[: len(args)]
        made = refs[len(args) + len(after) :][: len(outs)]
        held = refs[len(args) + len(after) + len(outs) :]
        if not pinned:
            body(*ins, *made, *held)
            return
        first, sem = held[-2:]
        body(*ins, first, *made[1:], *held[:-2])
        copy_all([(first, made[0])], sem)

    out_specs = [slow if hbm_out or (pinned and i == 0) else fast for i in range(len(outs))]
    shapes = [
        pltpu.HBM(o.shape, o.dtype) if hbm_out or (pinned and i == 0) else o
        for i, o in enumerate(outs)
    ]
    return pl.pallas_call(
        ordered,
        out_shape=shapes,
        in_specs=[slow if hbm_in else fast] * len(args) + [pl.BlockSpec(memory_space=pl.ANY)] * len(after),
        out_specs=out_specs,
        scratch_shapes=scratch,
        compiler_params=pltpu.CompilerParams(vmem_limit_bytes=16 * 1024 * 1024),
        cost_estimate=pl.CostEstimate(flops=flops, bytes_accessed=size, transcendentals=0),
    )(*[held_in_hbm(a) if hbm_in else a for a in args], *after)


def copy_all(pairs, sems):
    copies = [pltpu.make_async_copy(a, b, sems.at[i]) for i, (a, b) in enumerate(pairs)]
    for c in copies:
        c.start()
    for c in copies:
        c.wait()


def dot(a, b, dims):
    return lax.dot_general(a, b, dims, preferred_element_type=F32)


def pieces(x):
    hi = x.astype(BF16)
    lo = (x - hi.astype(F32)).astype(BF16)
    return hi, lo


def pieces3(x):
    hi = x.astype(BF16)
    mid, lo = pieces(x - hi.astype(F32))
    return [hi, mid, lo]


def exact_rows(row, mat, dims):
    stack = jnp.concatenate(pieces3(row), axis=0)
    return jnp.sum(dot(stack, mat, dims), axis=0, keepdims=True)


def send_half(a_ref, b_ref, send_ref, sems):
    there = 1 - lax.axis_index("c")
    size = send_ref.shape[1]
    part = pl.ds(pl.multiple_of(there * size, 16), size)
    copy_all([(a_ref.at[part], send_ref.at[0]), (b_ref.at[part], send_ref.at[1])], sems)


def merge_half(qm, qt, km, kt, q_ref, k_ref, v_ref):
    core = lax.axis_index("c")
    size = qm.shape[0]
    mine = pl.ds(pl.multiple_of(core * size, 16), size)
    theirs = pl.ds(pl.multiple_of((1 - core) * size, 16), size)
    q_ref[mine] = qm[...]
    q_ref[theirs] = qt[...]
    k_ref[mine] = km[0]
    k_ref[theirs] = kt[0]
    v_ref[mine] = km[1]
    v_ref[theirs] = kt[1]


def head_of(ref, got, i, h):
    start = lax.axis_index("c") * (HALF * HD) + h * HD
    own = ref[pl.ds(pl.multiple_of(start, 16), HD)]
    return jnp.concatenate([own, got[i, h * HD : (h + 1) * HD]], axis=1)


def columns(rows):
    wide = jnp.concatenate([rows, jnp.zeros((HALF, LANES - HD), F32)], axis=1)
    tall = jnp.concatenate([wide, jnp.zeros((8 - HALF, LANES), F32)], axis=0)
    return jnp.transpose(tall)


def spread(row, n):
    return jnp.broadcast_to(row[None], (n, 1, HD))


def sum_of(got, n, first, last):
    total = got[0, first:last]
    for j in range(1, n):
        total = total + got[j, first:last]
    return total


def state_body(n, rows, k_ref, v_ref, kv_got, pay, whole):
    for h in range(HALF):
        key = jnp.maximum(head_of(k_ref, kv_got, 0, h), 0)
        val = head_of(v_ref, kv_got, 1, h)
        whole[h * HD : (h + 1) * HD] = dot(key, val, NT)
        norm = dot(jnp.ones((8, key.shape[1]), BF16), key, NT)[:1]
        pay[:, rows + h : rows + h + 1] = spread(norm, n)
    for j in range(n):
        pay[j, :rows] = whole[j * rows : (j + 1) * rows]


def grad_body(n, rows, scale, got, q_ref, g_ref, qg_got, pay, norm_ref, inv_ref, whole):
    total = sum_of(got, n, 0, rows + HALF)
    norm_ref[...] = total[rows:]
    for h in range(HALF):
        query = jnp.maximum(head_of(q_ref, qg_got, 0, h), 0)
        grad = head_of(g_ref, qg_got, 1, h)
        inv = 1.0 / (exact_rows(total[rows + h : rows + h + 1], query, NN) + EPSILON)
        inv_ref[h : h + 1] = inv
        hi, lo = pieces(grad.astype(F32) * (inv * scale))
        whole[h * HD : (h + 1) * HD] = dot(query, hi, NT) + dot(query, lo, NT)
    shard = total[:rows]
    for j in range(n):
        pay[j, :rows] = shard
        pay[j, rows : 2 * rows] = whole[j * rows : (j + 1) * rows]


def query_body(
    n, rows, scale, got, q_ref, g_ref, qg_got, norm_ref, inv_ref, pay, out_mine, out_theirs, whole
):
    total = sum_of(got, n, rows, 2 * rows)
    for j in range(n):
        whole[j * rows : (j + 1) * rows] = got[j, :rows]
        pay[j, :rows] = total
    norms = columns(norm_ref[...])
    tok = out_mine.shape[1]
    for h in range(HALF):
        part = slice(h * HD, (h + 1) * HD)
        feat = jnp.maximum(head_of(q_ref, qg_got, 0, h), 0)
        query = feat.astype(F32)
        grad = head_of(g_ref, qg_got, 1, h)
        hi, lo = pieces(whole[part])
        prod = dot(hi, grad, NN) + dot(lo, grad, NN)
        inv = inv_ref[h : h + 1]
        weight = inv * scale
        proj = jnp.sum(query * prod, axis=0, keepdims=True) * weight * inv
        pay[:, rows + h : rows + h + 1] = spread(-exact_rows(proj, feat, NT), n)
        out = prod * weight - norms[:HD, h : h + 1] * proj
        out = jnp.where(query > 0, out, 0.0).astype(BF16)
        out_mine[part] = out[:, :tok]
        out_theirs[part] = out[:, tok:]


def key_body(n, rows, got, k_ref, v_ref, kv_got, out_mine, out_theirs, whole):
    for j in range(n):
        whole[j * rows : (j + 1) * rows] = got[j, :rows]
    norms = columns(sum_of(got, n, rows, rows + HALF))
    tok = out_mine.shape[2]
    for h in range(HALF):
        part = slice(h * HD, (h + 1) * HD)
        key = head_of(k_ref, kv_got, 0, h)
        val = head_of(v_ref, kv_got, 1, h)
        hi, lo = pieces(whole[part])
        k_out = dot(hi, val, NN) + dot(lo, val, NN) + norms[:HD, h : h + 1]
        k_out = jnp.where(key.astype(F32) > 0, k_out, 0.0).astype(BF16)
        feat = jnp.maximum(key, 0)
        v_out = (dot(hi, feat, TN) + dot(lo, feat, TN)).astype(BF16)
        out_mine[0, part] = k_out[:, :tok]
        out_theirs[0, part] = k_out[:, tok:]
        out_mine[1, part] = v_out[:, :tok]
        out_theirs[1, part] = v_out[:, tok:]


def shift(x, step):
    rows = lax.broadcasted_iota(jnp.int32, x.shape, 0)
    moved = pltpu.roll(x, step % x.shape[0], 0)
    edge = 0 if step > 0 else x.shape[0] - 1
    return jnp.where(rows == edge, 0.0, moved)


def taps(sources, weight, picks, lanes):
    planes = [ref[:, lanes].astype(F32) for ref in sources]

    def column(j):
        return sum(p * weight[i, pl.ds(j, 1), lanes] for p, i in zip(planes, picks))

    return (column(1) + shift(column(0), -1) + shift(column(2), 1)).astype(BF16)


def halve_body(row, weight, mine, send, weight_mine, sems):
    side = lax.axis_index("x")
    width = mine.shape[1]
    here = pl.ds(pl.multiple_of(side * width, LANES), width)
    there = pl.ds(pl.multiple_of((1 - side) * width, LANES), width)
    pairs = [
        (row.at[0, 0, :, there], send),
        (row.at[0, 0, :, here], mine),
        (weight.at[:, :, here], weight_mine),
    ]
    copy_all(pairs, sems)


def send_body(mine, got, far, weight, out, token):
    token[...] = jnp.zeros(token.shape, F32)
    side = lax.axis_index("x")
    width = mine.shape[1]

    @pl.loop(0, width // LANES)
    def _(t):
        lanes = pl.ds(pl.multiple_of(t * LANES, LANES), LANES)
        out[:, lanes] = taps((got, mine, far), weight, (1, 2 - 2 * side, 2 * side), lanes)


def keep_body(mine, got, far, back, weight, out, token):
    token[...] = jnp.zeros(token.shape, F32)
    side = lax.axis_index("x")
    width = mine.shape[1]

    @pl.loop(0, width // LANES)
    def _(t):
        at = t * LANES
        lanes = pl.ds(pl.multiple_of(at, LANES), LANES)
        here = pl.ds(pl.multiple_of(side * width + at, LANES), LANES)
        there = pl.ds(pl.multiple_of((1 - side) * width + at, LANES), LANES)
        out[0, 0, :, here] = taps((mine, got, far), weight, (1, 2 * side, 2 - 2 * side), lanes)
        out[0, 0, :, there] = back[:, lanes]


def shards(queries, key_proj, value_proj, attn_grad, conv_grad, conv_weight):
    tok = queries.shape[0] * queries.shape[1] * queries.shape[2]
    tokens_all = tok * lax.axis_size(("y", "c", "z", "x"))
    scale = math.sqrt(tokens_all)
    n = lax.axis_size(CHIPS)
    rows = -(-HALF * HD // n)
    pay_one = -(-(rows + HALF) // 8) * 8
    pay_two = -(-2 * rows // 8) * 8
    swap = [(0, 1), (1, 0)]
    two_sems = [pltpu.SemaphoreType.DMA((2,))]
    sd = jax.ShapeDtypeStruct
    scratch = [pltpu.VMEM((n * rows, HD), F32)]
    half = HALF * HD
    pair_shape = sd((2, half, tok), BF16)
    q, k, v, g = (
        jnp.swapaxes(a, 2, 3).reshape(2 * half, tok)
        for a in (queries, key_proj, value_proj, attn_grad)
    )

    z_size = lax.axis_size("z")
    ahead = [(z, z + 1) for z in range(z_size - 1)]
    even_up = [(2 * i, 2 * j) for i, j in ahead]
    even_down = [(2 * j, 2 * i) for i, j in ahead]
    odd_up = [(2 * i + 1, 2 * j + 1) for i, j in ahead]
    odd_down = [(2 * j + 1, 2 * i + 1) for i, j in ahead]
    cols, ch = conv_grad.shape[2:]
    width = ch // 2
    half_shape = sd((cols, width), BF16)
    token = sd((8, LANES), F32)
    row_mine, row_send, weight = call(
        halve_body,
        [half_shape, half_shape, sd((3, 3, width), F32)],
        (conv_grad, conv_weight),
        [pltpu.SemaphoreType.DMA((3,))],
        hbm_in=True,
        hbm_out=True,
    )
    row_got = lax.ppermute(row_send, "x", swap)
    far_own = lax.ppermute(row_mine, ("z", "x"), even_down + odd_up)
    far_fwd = lax.ppermute(row_got, ("z", "x"), even_up + odd_down)
    out_send, sent = call(
        send_body,
        [half_shape, token],
        (row_mine, row_got, far_own, weight),
        flops=20 * cols * width,
    )
    out_got = lax.ppermute(out_send, "x", swap)
    input_grad, kept = call(
        keep_body,
        [sd(conv_grad.shape, BF16), token],
        (row_mine, row_got, far_fwd, out_got, weight),
        flops=20 * cols * width,
    )

    kv_send = call(send_half, [pair_shape], (k, v), two_sems, hbm_in=True, hbm_out=True)[0]
    kv_got = lax.ppermute(kv_send, "c", swap)
    qg_send = call(send_half, [pair_shape], (q, g), two_sems, hbm_in=True, hbm_out=True)[0]
    qg_got = lax.ppermute(qg_send, "c", swap)

    def exchange(pay):
        return lax.all_to_all(pay, CHIPS, split_axis=0, concat_axis=0, tiled=True)

    macs = HALF * 2 * tok * HD * HD
    (pay,) = call(
        functools.partial(state_body, n, rows),
        [sd((n, pay_one, HD), F32)],
        (k, v, kv_got),
        scratch,
        flops=2 * macs,
        pinned=True,
    )
    got = exchange(pay)
    pay, norm, inv = call(
        functools.partial(grad_body, n, rows, scale),
        [sd((n, pay_two, HD), F32), sd((HALF, HD), F32), sd((HALF, 2 * tok), F32)],
        (got, q, g, qg_got),
        scratch,
        flops=4 * macs,
        pinned=True,
        after=(row_got, far_own),
    )
    got = exchange(pay)
    pay, query_mine, query_send = call(
        functools.partial(query_body, n, rows, scale),
        [sd((n, pay_one, HD), F32)] + [sd((half, tok), BF16)] * 2,
        (got, q, g, qg_got, norm, inv),
        scratch,
        flops=4 * macs,
        pinned=True,
        after=(sent,),
    )
    query_got = lax.ppermute(query_send, "c", swap)
    got = exchange(pay)
    key_mine, key_send = call(
        functools.partial(key_body, n, rows),
        [pair_shape] * 2,
        (got, k, v, kv_got),
        scratch,
        flops=8 * macs,
        after=(kept,),
    )
    key_got = lax.ppermute(key_send, "c", swap)
    outs = call(
        merge_half,
        [sd((2 * half, tok), BF16)] * 3,
        (query_mine, query_got, key_mine, key_got),
    )
    outs = [jnp.swapaxes(o.reshape(*queries.shape[:2], 2 * half, -1), 2, 3) for o in outs]
    return (*outs, input_grad)


def solution(mesh):
    frames, bands = mesh.shape["frame"], mesh.shape["row"]
    fine = Mesh(mesh.devices.reshape(frames // 2, 2, bands // 2, 2), ("y", "c", "z", "x"))
    split = P(("y", "c"), ("z", "x"), None, None)
    return jax.shard_map(
        shards,
        mesh=fine,
        in_specs=(split,) * 5 + (P(),),
        out_specs=(split,) * 4,
        check_vma=False,
    )
```

```python
import functools
import math

import jax
import jax.numpy as jnp
from jax import lax
from jax.experimental import pallas as pl
from jax.experimental.pallas import tpu as pltpu
from jax.sharding import Mesh, PartitionSpec as P

HEADS = 10
HD = 112
EPSILON = 1e-06
HALF = HEADS // 2
LANES = 128
CHIPS = ("y", "z", "x")
F32 = jnp.float32
BF16 = jnp.bfloat16

NT = (((1,), (1,)), ((), ()))
TN = (((0,), (0,)), ((), ()))
NN = (((1,), (0,)), ((), ()))


def held_in_hbm(x):
    return pltpu.with_memory_space_constraint(x, pltpu.HBM)


def call(body, outs, args, scratch=(), flops=0, after=(), hbm_in=False, hbm_out=False, pinned=False):
    size = sum(math.prod(a.shape) * a.dtype.itemsize for a in list(args) + list(outs))
    fast = pl.BlockSpec(memory_space=pltpu.VMEM)
    slow = pl.BlockSpec(memory_space=pltpu.HBM)
    scratch = list(scratch)
    if pinned:
        scratch += [pltpu.VMEM(outs[0].shape, outs[0].dtype), pltpu.SemaphoreType.DMA((1,))]

    def ordered(*refs):
        ins = refs[: len(args)]
        made = refs[len(args) + len(after) :][: len(outs)]
        held = refs[len(args) + len(after) + len(outs) :]
        if not pinned:
            body(*ins, *made, *held)
            return
        first, sem = held[-2:]
        body(*ins, first, *made[1:], *held[:-2])
        copy_all([(first, made[0])], sem)

    out_specs = [slow if hbm_out or (pinned and i == 0) else fast for i in range(len(outs))]
    shapes = [
        pltpu.HBM(o.shape, o.dtype) if hbm_out or (pinned and i == 0) else o
        for i, o in enumerate(outs)
    ]
    return pl.pallas_call(
        ordered,
        out_shape=shapes,
        in_specs=[slow if hbm_in else fast] * len(args) + [pl.BlockSpec(memory_space=pl.ANY)] * len(after),
        out_specs=out_specs,
        scratch_shapes=scratch,
        compiler_params=pltpu.CompilerParams(vmem_limit_bytes=16 * 1024 * 1024),
        cost_estimate=pl.CostEstimate(flops=flops, bytes_accessed=size, transcendentals=0),
    )(*[held_in_hbm(a) if hbm_in else a for a in args], *after)


def copy_all(pairs, sems):
    copies = [pltpu.make_async_copy(a, b, sems.at[i]) for i, (a, b) in enumerate(pairs)]
    for c in copies:
        c.start()
    for c in copies:
        c.wait()


def dot(a, b, dims):
    return lax.dot_general(a, b, dims, preferred_element_type=F32)


def pieces(x):
    hi = x.astype(BF16)
    lo = (x - hi.astype(F32)).astype(BF16)
    return hi, lo


def pieces3(x):
    hi = x.astype(BF16)
    mid, lo = pieces(x - hi.astype(F32))
    return [hi, mid, lo]


def exact_rows(row, mat, dims):
    stack = jnp.concatenate(pieces3(row), axis=0)
    return jnp.sum(dot(stack, mat, dims), axis=0, keepdims=True)


def send_half(a_ref, b_ref, send_ref, sems):
    there = 1 - lax.axis_index("c")
    size = send_ref.shape[1]
    part = pl.ds(pl.multiple_of(there * size, 16), size)
    copy_all([(a_ref.at[part], send_ref.at[0]), (b_ref.at[part], send_ref.at[1])], sems)


def merge_half(qm, qt, km, kt, q_ref, k_ref, v_ref):
    core = lax.axis_index("c")
    size = qm.shape[0]
    mine = pl.ds(pl.multiple_of(core * size, 16), size)
    theirs = pl.ds(pl.multiple_of((1 - core) * size, 16), size)
    q_ref[mine] = qm[...]
    q_ref[theirs] = qt[...]
    k_ref[mine] = km[0]
    k_ref[theirs] = kt[0]
    v_ref[mine] = km[1]
    v_ref[theirs] = kt[1]


def head_of(ref, got, i, h):
    start = lax.axis_index("c") * (HALF * HD) + h * HD
    own = ref[pl.ds(pl.multiple_of(start, 16), HD)]
    return jnp.concatenate([own, got[i, h * HD : (h + 1) * HD]], axis=1)


def columns(rows):
    wide = jnp.concatenate([rows, jnp.zeros((HALF, LANES - HD), F32)], axis=1)
    tall = jnp.concatenate([wide, jnp.zeros((8 - HALF, LANES), F32)], axis=0)
    return jnp.transpose(tall)


def spread(row, n):
    return jnp.broadcast_to(row[None], (n, 1, HD))


def sum_of(got, n, first, last):
    total = got[0, first:last]
    for j in range(1, n):
        total = total + got[j, first:last]
    return total


def state_body(n, rows, k_ref, v_ref, kv_got, pay, whole):
    for h in range(HALF):
        key = jnp.maximum(head_of(k_ref, kv_got, 0, h), 0)
        val = head_of(v_ref, kv_got, 1, h)
        whole[h * HD : (h + 1) * HD] = dot(key, val, NT)
        norm = dot(jnp.ones((8, key.shape[1]), BF16), key, NT)[:1]
        pay[:, rows + h : rows + h + 1] = spread(norm, n)
    for j in range(n):
        pay[j, :rows] = whole[j * rows : (j + 1) * rows]


def grad_body(n, rows, scale, got, q_ref, g_ref, qg_got, pay, norm_ref, inv_ref, whole):
    total = sum_of(got, n, 0, rows + HALF)
    norm_ref[...] = total[rows:]
    for h in range(HALF):
        query = jnp.maximum(head_of(q_ref, qg_got, 0, h), 0)
        grad = head_of(g_ref, qg_got, 1, h)
        inv = 1.0 / (exact_rows(total[rows + h : rows + h + 1], query, NN) + EPSILON)
        inv_ref[h : h + 1] = inv
        hi, lo = pieces(grad.astype(F32) * (inv * scale))
        whole[h * HD : (h + 1) * HD] = dot(query, hi, NT) + dot(query, lo, NT)
    shard = total[:rows]
    for j in range(n):
        pay[j, :rows] = shard
        pay[j, rows : 2 * rows] = whole[j * rows : (j + 1) * rows]


def query_body(
    n, rows, scale, got, q_ref, g_ref, qg_got, norm_ref, inv_ref, pay, out_mine, out_theirs, whole
):
    total = sum_of(got, n, rows, 2 * rows)
    for j in range(n):
        whole[j * rows : (j + 1) * rows] = got[j, :rows]
        pay[j, :rows] = total
    norms = columns(norm_ref[...])
    tok = out_mine.shape[1]
    for h in range(HALF):
        part = slice(h * HD, (h + 1) * HD)
        feat = jnp.maximum(head_of(q_ref, qg_got, 0, h), 0)
        query = feat.astype(F32)
        grad = head_of(g_ref, qg_got, 1, h)
        hi, lo = pieces(whole[part])
        prod = dot(hi, grad, NN) + dot(lo, grad, NN)
        inv = inv_ref[h : h + 1]
        weight = inv * scale
        proj = jnp.sum(query * prod, axis=0, keepdims=True) * weight * inv
        pay[:, rows + h : rows + h + 1] = spread(-exact_rows(proj, feat, NT), n)
        out = prod * weight - norms[:HD, h : h + 1] * proj
        out = jnp.where(query > 0, out, 0.0).astype(BF16)
        out_mine[part] = out[:, :tok]
        out_theirs[part] = out[:, tok:]


def key_body(n, rows, got, k_ref, v_ref, kv_got, out_mine, out_theirs, whole):
    for j in range(n):
        whole[j * rows : (j + 1) * rows] = got[j, :rows]
    norms = columns(sum_of(got, n, rows, rows + HALF))
    tok = out_mine.shape[2]
    for h in range(HALF):
        part = slice(h * HD, (h + 1) * HD)
        key = head_of(k_ref, kv_got, 0, h)
        val = head_of(v_ref, kv_got, 1, h)
        hi, lo = pieces(whole[part])
        k_out = dot(hi, val, NN) + dot(lo, val, NN) + norms[:HD, h : h + 1]
        k_out = jnp.where(key.astype(F32) > 0, k_out, 0.0).astype(BF16)
        feat = jnp.maximum(key, 0)
        v_out = (dot(hi, feat, TN) + dot(lo, feat, TN)).astype(BF16)
        out_mine[0, part] = k_out[:, :tok]
        out_theirs[0, part] = k_out[:, tok:]
        out_mine[1, part] = v_out[:, :tok]
        out_theirs[1, part] = v_out[:, tok:]


def shift(x, step):
    rows = lax.broadcasted_iota(jnp.int32, x.shape, 0)
    moved = pltpu.roll(x, step % x.shape[0], 0)
    edge = 0 if step > 0 else x.shape[0] - 1
    return jnp.where(rows == edge, 0.0, moved)


def taps(sources, weight, picks, lanes):
    planes = [ref[:, lanes].astype(F32) for ref in sources]

    def column(j):
        return sum(p * weight[i, pl.ds(j, 1), lanes] for p, i in zip(planes, picks))

    return (column(1) + shift(column(0), -1) + shift(column(2), 1)).astype(BF16)


def halve_body(row, weight, mine, send, weight_mine, sems):
    side = lax.axis_index("x")
    width = mine.shape[1]
    here = pl.ds(pl.multiple_of(side * width, LANES), width)
    there = pl.ds(pl.multiple_of((1 - side) * width, LANES), width)
    pairs = [
        (row.at[0, 0, :, there], send),
        (row.at[0, 0, :, here], mine),
        (weight.at[:, :, here], weight_mine),
    ]
    copy_all(pairs, sems)


def send_body(mine, got, far, weight, out, token):
    token[...] = jnp.zeros(token.shape, F32)
    side = lax.axis_index("x")
    width = mine.shape[1]

    @pl.loop(0, width // LANES)
    def _(t):
        lanes = pl.ds(pl.multiple_of(t * LANES, LANES), LANES)
        out[:, lanes] = taps((got, mine, far), weight, (1, 2 - 2 * side, 2 * side), lanes)


def keep_body(mine, got, far, back, weight, out, token):
    token[...] = jnp.zeros(token.shape, F32)
    side = lax.axis_index("x")
    width = mine.shape[1]

    @pl.loop(0, width // LANES)
    def _(t):
        at = t * LANES
        lanes = pl.ds(pl.multiple_of(at, LANES), LANES)
        here = pl.ds(pl.multiple_of(side * width + at, LANES), LANES)
        there = pl.ds(pl.multiple_of((1 - side) * width + at, LANES), LANES)
        out[0, 0, :, here] = taps((mine, got, far), weight, (1, 2 * side, 2 - 2 * side), lanes)
        out[0, 0, :, there] = back[:, lanes]


def shards(queries, key_proj, value_proj, attn_grad, conv_grad, conv_weight):
    tok = queries.shape[0] * queries.shape[1] * queries.shape[2]
    tokens_all = tok * lax.axis_size(("y", "c", "z", "x"))
    scale = math.sqrt(tokens_all)
    n = lax.axis_size(CHIPS)
    rows = -(-HALF * HD // n)
    pay_one = -(-(rows + HALF) // 8) * 8
    pay_two = -(-2 * rows // 8) * 8
    swap = [(0, 1), (1, 0)]
    two_sems = [pltpu.SemaphoreType.DMA((2,))]
    sd = jax.ShapeDtypeStruct
    scratch = [pltpu.VMEM((n * rows, HD), F32)]
    half = HALF * HD
    pair_shape = sd((2, half, tok), BF16)
    q, k, v, g = (
        jnp.swapaxes(a, 2, 3).reshape(2 * half, tok)
        for a in (queries, key_proj, value_proj, attn_grad)
    )

    z_size = lax.axis_size("z")
    ahead = [(z, z + 1) for z in range(z_size - 1)]
    even_up = [(2 * i, 2 * j) for i, j in ahead]
    even_down = [(2 * j, 2 * i) for i, j in ahead]
    odd_up = [(2 * i + 1, 2 * j + 1) for i, j in ahead]
    odd_down = [(2 * j + 1, 2 * i + 1) for i, j in ahead]
    cols, ch = conv_grad.shape[2:]
    width = ch // 2
    half_shape = sd((cols, width), BF16)
    token = sd((8, LANES), F32)
    row_mine, row_send, weight = call(
        halve_body,
        [half_shape, half_shape, sd((3, 3, width), F32)],
        (conv_grad, conv_weight),
        [pltpu.SemaphoreType.DMA((3,))],
        hbm_in=True,
    )
    row_got = lax.ppermute(row_send, "x", swap)
    far_own = lax.ppermute(row_mine, ("z", "x"), even_down + odd_up)
    far_fwd = lax.ppermute(row_got, ("z", "x"), even_up + odd_down)
    out_send, sent = call(
        send_body,
        [half_shape, token],
        (row_mine, row_got, far_own, weight),
        flops=20 * cols * width,
    )
    out_got = lax.ppermute(out_send, "x", swap)
    input_grad, kept = call(
        keep_body,
        [sd(conv_grad.shape, BF16), token],
        (row_mine, row_got, far_fwd, out_got, weight),
        flops=20 * cols * width,
    )

    kv_send = call(send_half, [pair_shape], (k, v), two_sems, hbm_in=True)[0]
    kv_got = lax.ppermute(kv_send, "c", swap)
    qg_send = call(send_half, [pair_shape], (q, g), two_sems, hbm_in=True)[0]
    qg_got = lax.ppermute(qg_send, "c", swap)

    def exchange(pay):
        return lax.all_to_all(pay, CHIPS, split_axis=0, concat_axis=0, tiled=True)

    macs = HALF * 2 * tok * HD * HD
    (pay,) = call(
        functools.partial(state_body, n, rows),
        [sd((n, pay_one, HD), F32)],
        (k, v, kv_got),
        scratch,
        flops=2 * macs,
        pinned=True,
    )
    got = exchange(pay)
    pay, norm, inv = call(
        functools.partial(grad_body, n, rows, scale),
        [sd((n, pay_two, HD), F32), sd((HALF, HD), F32), sd((HALF, 2 * tok), F32)],
        (got, q, g, qg_got),
        scratch,
        flops=4 * macs,
        pinned=True,
        after=(row_got, far_own),
    )
    got = exchange(pay)
    pay, query_mine, query_send = call(
        functools.partial(query_body, n, rows, scale),
        [sd((n, pay_one, HD), F32)] + [sd((half, tok), BF16)] * 2,
        (got, q, g, qg_got, norm, inv),
        scratch,
        flops=4 * macs,
        pinned=True,
        after=(sent,),
    )
    query_got = lax.ppermute(query_send, "c", swap)
    got = exchange(pay)
    key_mine, key_send = call(
        functools.partial(key_body, n, rows),
        [pair_shape] * 2,
        (got, k, v, kv_got),
        scratch,
        flops=8 * macs,
        after=(kept,),
    )
    key_got = lax.ppermute(key_send, "c", swap)
    outs = call(
        merge_half,
        [sd((2 * half, tok), BF16)] * 3,
        (query_mine, query_got, key_mine, key_got),
    )
    outs = [jnp.swapaxes(o.reshape(*queries.shape[:2], 2 * half, -1), 2, 3) for o in outs]
    return (*outs, input_grad)


def solution(mesh):
    frames, bands = mesh.shape["frame"], mesh.shape["row"]
    fine = Mesh(mesh.devices.reshape(frames // 2, 2, bands // 2, 2), ("y", "c", "z", "x"))
    split = P(("y", "c"), ("z", "x"), None, None)
    return jax.shard_map(
        shards,
        mesh=fine,
        in_specs=(split,) * 5 + (P(),),
        out_specs=(split,) * 4,
        check_vma=False,
    )
```

```python
import functools
import math

import jax
import jax.numpy as jnp
from jax import lax
from jax.experimental import pallas as pl
from jax.experimental.pallas import tpu as pltpu
from jax.sharding import Mesh, PartitionSpec as P

HEADS = 10
HD = 112
EPSILON = 1e-06
HALF = HEADS // 2
LANES = 128
CHUNKS = 2
CHIPS = ("y", "z", "x")
F32 = jnp.float32
BF16 = jnp.bfloat16

NT = (((1,), (1,)), ((), ()))
TN = (((0,), (0,)), ((), ()))
NN = (((1,), (0,)), ((), ()))


def held_in_hbm(x):
    return pltpu.with_memory_space_constraint(x, pltpu.HBM)


def call(body, outs, args, scratch=(), flops=0, after=(), any_in=False, hbm_out=0, pinned=False, alias=None):
    size = sum(math.prod(a.shape) * a.dtype.itemsize for a in list(args) + list(outs))
    fast = pl.BlockSpec(memory_space=pltpu.VMEM)
    slow = pl.BlockSpec(memory_space=pltpu.HBM)
    free = pl.BlockSpec(memory_space=pl.ANY)
    scratch = list(scratch)
    if pinned:
        scratch += [pltpu.VMEM(outs[0].shape, outs[0].dtype), pltpu.SemaphoreType.DMA((1,))]

    def ordered(*refs):
        ins = refs[: len(args)]
        made = refs[len(args) + len(after) :][: len(outs)]
        held = refs[len(args) + len(after) + len(outs) :]
        if not pinned:
            body(*ins, *made, *held)
            return
        first, sem = held[-2:]
        body(*ins, first, *made[1:], *held[:-2])
        copy_all([(first, made[0])], sem)

    out_specs = [slow if i < max(hbm_out, pinned) else fast for i in range(len(outs))]
    shapes = [
        pltpu.HBM(o.shape, o.dtype) if i < max(hbm_out, pinned) else o
        for i, o in enumerate(outs)
    ]
    return pl.pallas_call(
        ordered,
        out_shape=shapes,
        in_specs=[free if any_in else fast] * len(args) + [free] * len(after),
        out_specs=out_specs,
        scratch_shapes=scratch,
        compiler_params=pltpu.CompilerParams(vmem_limit_bytes=16 * 1024 * 1024),
        cost_estimate=pl.CostEstimate(flops=flops, bytes_accessed=size, transcendentals=0),
        input_output_aliases=alias or {},
    )(*args, *after)


def copy_all(pairs, sems):
    copies = [pltpu.make_async_copy(a, b, sems.at[i]) for i, (a, b) in enumerate(pairs)]
    for c in copies:
        c.start()
    for c in copies:
        c.wait()


def dot(a, b, dims):
    return lax.dot_general(a, b, dims, preferred_element_type=F32)


def pieces(x):
    hi = x.astype(BF16)
    lo = (x - hi.astype(F32)).astype(BF16)
    return hi, lo


def pieces3(x):
    hi = x.astype(BF16)
    mid, lo = pieces(x - hi.astype(F32))
    return [hi, mid, lo]


def exact_rows(row, mat, dims):
    stack = jnp.concatenate(pieces3(row), axis=0)
    return jnp.sum(dot(stack, mat, dims), axis=0, keepdims=True)


def send_half(a_ref, b_ref, send_ref, sems):
    there = 1 - lax.axis_index("c")
    size = send_ref.shape[1]
    part = pl.ds(pl.multiple_of(there * size, 16), size)
    copy_all([(a_ref.at[part], send_ref.at[0]), (b_ref.at[part], send_ref.at[1])], sems)


def halves(size):
    core = lax.axis_index("c")
    mine = pl.ds(pl.multiple_of(core * size, 16), size)
    theirs = pl.ds(pl.multiple_of((1 - core) * size, 16), size)
    return mine, theirs


def merge_query(own, far, out, token):
    token[...] = jnp.zeros(token.shape, F32)
    mine, theirs = halves(own.shape[0])
    out[mine] = own[...]
    out[theirs] = far[...]


def merge_pair(own, far, first, second):
    mine, theirs = halves(own.shape[1])
    for i, out in enumerate((first, second)):
        out[mine] = own[i]
        out[theirs] = far[i]


def head_of(ref, got, i, h):
    start = lax.axis_index("c") * (HALF * HD) + h * HD
    own = ref[pl.ds(pl.multiple_of(start, 16), HD)]
    return jnp.concatenate([own, got[i, h * HD : (h + 1) * HD]], axis=1)


def columns(rows):
    wide = jnp.concatenate([rows, jnp.zeros((HALF, LANES - HD), F32)], axis=1)
    tall = jnp.concatenate([wide, jnp.zeros((8 - HALF, LANES), F32)], axis=0)
    return jnp.transpose(tall)


def spread(row, n):
    return jnp.broadcast_to(row[None], (n, 1, HD))


def sum_of(got, n, first, last):
    total = got[0, first:last]
    for j in range(1, n):
        total = total + got[j, first:last]
    return total


def state_body(n, rows, k_ref, v_ref, kv_got, pay, token, whole):
    token[...] = jnp.zeros(token.shape, F32)
    for h in range(HALF):
        key = jnp.maximum(head_of(k_ref, kv_got, 0, h), 0)
        val = head_of(v_ref, kv_got, 1, h)
        whole[h * HD : (h + 1) * HD] = dot(key, val, NT)
        norm = dot(jnp.ones((8, key.shape[1]), BF16), key, NT)[:1]
        pay[:, rows + h : rows + h + 1] = spread(norm, n)
    for j in range(n):
        pay[j, :rows] = whole[j * rows : (j + 1) * rows]


def grad_body(n, rows, scale, got, q_ref, g_ref, qg_got, pay, norm_ref, inv_ref, whole):
    total = sum_of(got, n, 0, rows + HALF)
    norm_ref[...] = total[rows:]
    for h in range(HALF):
        query = jnp.maximum(head_of(q_ref, qg_got, 0, h), 0)
        grad = head_of(g_ref, qg_got, 1, h)
        inv = 1.0 / (exact_rows(total[rows + h : rows + h + 1], query, NN) + EPSILON)
        inv_ref[h : h + 1] = inv
        hi, lo = pieces(grad.astype(F32) * (inv * scale))
        whole[h * HD : (h + 1) * HD] = dot(query, hi, NT) + dot(query, lo, NT)
    shard = total[:rows]
    for j in range(n):
        pay[j, :rows] = shard
        pay[j, rows : 2 * rows] = whole[j * rows : (j + 1) * rows]


def query_body(
    n, rows, scale, got, q_ref, g_ref, qg_got, norm_ref, inv_ref, pay, out_mine, out_theirs, whole
):
    total = sum_of(got, n, rows, 2 * rows)
    for j in range(n):
        whole[j * rows : (j + 1) * rows] = got[j, :rows]
        pay[j, :rows] = total
    norms = columns(norm_ref[...])
    tok = out_mine.shape[1]
    for h in range(HALF):
        part = slice(h * HD, (h + 1) * HD)
        feat = jnp.maximum(head_of(q_ref, qg_got, 0, h), 0)
        query = feat.astype(F32)
        grad = head_of(g_ref, qg_got, 1, h)
        hi, lo = pieces(whole[part])
        prod = dot(hi, grad, NN) + dot(lo, grad, NN)
        inv = inv_ref[h : h + 1]
        weight = inv * scale
        proj = jnp.sum(query * prod, axis=0, keepdims=True) * weight * inv
        pay[:, rows + h : rows + h + 1] = spread(-exact_rows(proj, feat, NT), n)
        out = prod * weight - norms[:HD, h : h + 1] * proj
        out = jnp.where(query > 0, out, 0.0).astype(BF16)
        out_mine[part] = out[:, :tok]
        out_theirs[part] = out[:, tok:]


def key_body(n, rows, got, k_ref, v_ref, kv_got, out_mine, out_theirs, whole):
    for j in range(n):
        whole[j * rows : (j + 1) * rows] = got[j, :rows]
    norms = columns(sum_of(got, n, rows, rows + HALF))
    tok = out_mine.shape[2]
    for h in range(HALF):
        part = slice(h * HD, (h + 1) * HD)
        key = head_of(k_ref, kv_got, 0, h)
        val = head_of(v_ref, kv_got, 1, h)
        hi, lo = pieces(whole[part])
        k_out = dot(hi, val, NN) + dot(lo, val, NN) + norms[:HD, h : h + 1]
        k_out = jnp.where(key.astype(F32) > 0, k_out, 0.0).astype(BF16)
        feat = jnp.maximum(key, 0)
        v_out = (dot(hi, feat, TN) + dot(lo, feat, TN)).astype(BF16)
        out_mine[0, part] = k_out[:, :tok]
        out_theirs[0, part] = k_out[:, tok:]
        out_mine[1, part] = v_out[:, :tok]
        out_theirs[1, part] = v_out[:, tok:]


def shift(x, step):
    rows = lax.broadcasted_iota(jnp.int32, x.shape, 0)
    moved = pltpu.roll(x, step % x.shape[0], 0)
    edge = 0 if step > 0 else x.shape[0] - 1
    return jnp.where(rows == edge, 0.0, moved)


def taps(sources, weight, picks, lanes, near):
    planes = [ref[:, lanes].astype(F32) for ref in sources]

    def column(j):
        return sum(p * weight[i, pl.ds(j, 1), near] for p, i in zip(planes, picks))

    return (column(1) + shift(column(0), -1) + shift(column(2), 1)).astype(BF16)


def columns_at(start, width):
    return pl.ds(pl.multiple_of(start, LANES), width)


def halve_body(row, weight, *refs):
    outs, token, held, sems = refs[:5], refs[5], refs[6:11], refs[11]
    token[...] = jnp.zeros(token.shape, F32)
    side = lax.axis_index("x")
    width = outs[0].shape[1]
    pairs = []
    for i in range(CHUNKS):
        send = columns_at((1 - side) * CHUNKS * width + i * width, width)
        mine = columns_at(side * CHUNKS * width + i * width, width)
        pairs += [row.at[0, 0, :, send], row.at[0, 0, :, mine]]
    pairs.append(weight.at[:, :, columns_at(side * CHUNKS * width, CHUNKS * width)])
    copy_all(list(zip(pairs, held)), sems)
    copy_all(list(zip(held, outs)), sems)


def send_body(at, mine, got, far, weight, out, token, *held):
    *held, made, sems = held
    token[...] = jnp.zeros(token.shape, F32)
    copy_all(list(zip((mine, got, far, weight), held)), sems)
    mine, got, far, weight = held
    side = lax.axis_index("x")
    width = mine.shape[1]

    @pl.loop(0, width // LANES)
    def _(t):
        lanes = columns_at(t * LANES, LANES)
        near = columns_at(at + t * LANES, LANES)
        made[:, lanes] = taps((got, mine, far), weight, (1, 2 - 2 * side, 2 * side), lanes, near)

    copy_all([(made, out)], sems)


def keep_body(at, mine, got, far, back, weight, *refs):
    out, token, *held = refs[-9:]
    *held, made, sems = held
    token[...] = jnp.zeros(token.shape, F32)
    copy_all(list(zip((mine, got, far, back, weight), held)), sems)
    mine, got, far, back, weight = held
    side = lax.axis_index("x")
    width = mine.shape[1]

    @pl.loop(0, width // LANES)
    def _(t):
        lanes = columns_at(t * LANES, LANES)
        near = columns_at(at + t * LANES, LANES)
        made[:, lanes] = taps((mine, got, far), weight, (1, 2 * side, 2 - 2 * side), lanes, near)

    here = columns_at(side * CHUNKS * width + at, width)
    there = columns_at((1 - side) * CHUNKS * width + at, width)
    copy_all([(made, out.at[0, 0, :, here]), (back, out.at[0, 0, :, there])], sems)


def shards(queries, key_proj, value_proj, attn_grad, conv_grad, conv_weight):
    tok = queries.shape[0] * queries.shape[1] * queries.shape[2]
    tokens_all = tok * lax.axis_size(("y", "c", "z", "x"))
    scale = math.sqrt(tokens_all)
    n = lax.axis_size(CHIPS)
    rows = -(-HALF * HD // n)
    pay_one = -(-(rows + HALF) // 8) * 8
    pay_two = -(-2 * rows // 8) * 8
    swap = [(0, 1), (1, 0)]
    two_sems = [pltpu.SemaphoreType.DMA((2,))]
    sd = jax.ShapeDtypeStruct
    scratch = [pltpu.VMEM((n * rows, HD), F32)]
    half = HALF * HD
    pair_shape = sd((2, half, tok), BF16)
    q, k, v, g = (
        jnp.swapaxes(a, 2, 3).reshape(2 * half, tok)
        for a in (queries, key_proj, value_proj, attn_grad)
    )

    z_size = lax.axis_size("z")
    ahead = [(z, z + 1) for z in range(z_size - 1)]
    even_up = [(2 * i, 2 * j) for i, j in ahead]
    even_down = [(2 * j, 2 * i) for i, j in ahead]
    odd_up = [(2 * i + 1, 2 * j + 1) for i, j in ahead]
    odd_down = [(2 * j + 1, 2 * i + 1) for i, j in ahead]
    cols, ch = conv_grad.shape[2:]
    width = ch // (2 * CHUNKS)
    half_shape = sd((cols, width), BF16)
    token = sd((8, LANES), F32)
    held = [pltpu.VMEM((cols, width), BF16)]
    held_weight = [pltpu.VMEM((3, 3, CHUNKS * width), F32)]

    def sems(count):
        return [pltpu.SemaphoreType.DMA((count,))]

    kv_send = call(send_half, [pair_shape], (held_in_hbm(k), held_in_hbm(v)), two_sems, any_in=True)[0]
    kv_got = lax.ppermute(kv_send, "c", swap)
    qg_send = call(send_half, [pair_shape], (held_in_hbm(q), held_in_hbm(g)), two_sems, any_in=True)[0]
    qg_got = lax.ppermute(qg_send, "c", swap)

    def exchange(pay):
        return lax.all_to_all(pay, CHIPS, split_axis=0, concat_axis=0, tiled=True)

    macs = HALF * 2 * tok * HD * HD
    pay, started = call(
        functools.partial(state_body, n, rows),
        [sd((n, pay_one, HD), F32), token],
        (k, v, kv_got),
        scratch,
        flops=2 * macs,
        pinned=True,
    )
    got = exchange(pay)
    *parts, weight, halved = call(
        halve_body,
        [half_shape] * (2 * CHUNKS) + [sd((3, 3, CHUNKS * width), F32), token],
        (held_in_hbm(conv_grad), held_in_hbm(conv_weight)),
        held * (2 * CHUNKS) + held_weight + sems(5),
        after=(started,),
        any_in=True,
        hbm_out=5,
    )
    row_send, row_mine = parts[::2], parts[1::2]

    def move_in(i):
        near = lax.ppermute(row_send[i], "x", swap)
        return near, lax.ppermute(row_mine[i], ("z", "x"), even_down + odd_up)

    def move_on(i, near, far):
        onward = lax.ppermute(near, ("z", "x"), even_up + odd_down)
        out_send, sent = call(
            functools.partial(send_body, i * width),
            [half_shape, token],
            (row_mine[i], near, far, weight),
            held * 3 + held_weight + held + sems(4),
            flops=20 * cols * width,
            any_in=True,
            hbm_out=1,
        )
        return onward, lax.ppermute(out_send, "x", swap), sent

    def finish(i, near, onward, back, before=()):
        return call(
            functools.partial(keep_body, i * width),
            [sd(conv_grad.shape, BF16), token],
            (row_mine[i], near, onward, back, weight, *before),
            held * 4 + held_weight + held + sems(5),
            flops=20 * cols * width,
            any_in=True,
            hbm_out=1,
            alias={5: 0} if before else None,
        )

    near_a, far_a = move_in(0)
    pay, norm, inv = call(
        functools.partial(grad_body, n, rows, scale),
        [sd((n, pay_two, HD), F32), sd((HALF, HD), F32), sd((HALF, 2 * tok), F32)],
        (got, q, g, qg_got),
        scratch,
        flops=4 * macs,
        pinned=True,
        after=(near_a, far_a),
    )
    near_b, far_b = move_in(1)
    onward_a, back_a, sent_a = move_on(0, near_a, far_a)
    got = exchange(pay)
    pay, query_mine, query_send = call(
        functools.partial(query_body, n, rows, scale),
        [sd((n, pay_one, HD), F32)] + [sd((half, tok), BF16)] * 2,
        (got, q, g, qg_got, norm, inv),
        scratch,
        flops=4 * macs,
        pinned=True,
        after=(near_b, far_b, sent_a),
    )
    query_got = lax.ppermute(query_send, "c", swap)
    onward_b, back_b, sent_b = move_on(1, near_b, far_b)
    input_grad, kept = finish(0, near_a, onward_a, back_a)
    whole_shape = sd((2 * half, tok), BF16)
    query_out, merged = call(merge_query, [whole_shape, token], (query_mine, query_got))
    got = exchange(pay)
    key_mine, key_send = call(
        functools.partial(key_body, n, rows),
        [pair_shape] * 2,
        (got, k, v, kv_got),
        scratch,
        flops=8 * macs,
        after=(kept, merged, sent_b),
    )
    key_got = lax.ppermute(key_send, "c", swap)
    input_grad, _ = finish(1, near_b, onward_b, back_b, (input_grad,))
    outs = query_out, *call(merge_pair, [whole_shape] * 2, (key_mine, key_got))
    outs = [jnp.swapaxes(o.reshape(*queries.shape[:2], 2 * half, -1), 2, 3) for o in outs]
    return (*outs, input_grad)


def solution(mesh):
    frames, bands = mesh.shape["frame"], mesh.shape["row"]
    fine = Mesh(mesh.devices.reshape(frames // 2, 2, bands // 2, 2), ("y", "c", "z", "x"))
    split = P(("y", "c"), ("z", "x"), None, None)
    return jax.shard_map(
        shards,
        mesh=fine,
        in_specs=(split,) * 5 + (P(),),
        out_specs=(split,) * 4,
        check_vma=False,
    )
```

```python
import functools
import math

import jax
import jax.numpy as jnp
from jax import lax
from jax.experimental import pallas as pl
from jax.experimental.pallas import tpu as pltpu
from jax.sharding import Mesh, PartitionSpec as P

HEADS = 10
HD = 112
EPSILON = 1e-06
HALF = HEADS // 2
LANES = 128
CUTS = (0,)
CHUNKS = 1
EARLY = 1
ORDER = [[('near', 0), ('far', 0), ('sent', 0)], [], [('kept', 0)]]
CHIPS = ("y", "z", "x")
F32 = jnp.float32
BF16 = jnp.bfloat16

NT = (((1,), (1,)), ((), ()))
TN = (((0,), (0,)), ((), ()))
NN = (((1,), (0,)), ((), ()))


def held_in_hbm(x):
    return pltpu.with_memory_space_constraint(x, pltpu.HBM)


def call(body, outs, args, scratch=(), flops=0, after=(), any_in=False, hbm_out=0, pinned=False, alias=None):
    size = sum(math.prod(a.shape) * a.dtype.itemsize for a in list(args) + list(outs))
    fast = pl.BlockSpec(memory_space=pltpu.VMEM)
    slow = pl.BlockSpec(memory_space=pltpu.HBM)
    free = pl.BlockSpec(memory_space=pl.ANY)
    scratch = list(scratch)
    if pinned:
        scratch += [pltpu.VMEM(outs[0].shape, outs[0].dtype), pltpu.SemaphoreType.DMA((1,))]

    def ordered(*refs):
        ins = refs[: len(args)]
        made = refs[len(args) + len(after) :][: len(outs)]
        held = refs[len(args) + len(after) + len(outs) :]
        if not pinned:
            body(*ins, *made, *held)
            return
        first, sem = held[-2:]
        body(*ins, first, *made[1:], *held[:-2])
        copy_all([(first, made[0])], sem)

    out_specs = [slow if i < max(hbm_out, pinned) else fast for i in range(len(outs))]
    shapes = [
        pltpu.HBM(o.shape, o.dtype) if i < max(hbm_out, pinned) else o
        for i, o in enumerate(outs)
    ]
    return pl.pallas_call(
        ordered,
        out_shape=shapes,
        in_specs=[free if any_in else fast] * len(args) + [free] * len(after),
        out_specs=out_specs,
        scratch_shapes=scratch,
        compiler_params=pltpu.CompilerParams(vmem_limit_bytes=16 * 1024 * 1024),
        cost_estimate=pl.CostEstimate(flops=flops, bytes_accessed=size, transcendentals=0),
        input_output_aliases=alias or {},
    )(*args, *after)


def copy_all(pairs, sems):
    copies = [pltpu.make_async_copy(a, b, sems.at[i]) for i, (a, b) in enumerate(pairs)]
    for c in copies:
        c.start()
    for c in copies:
        c.wait()


def dot(a, b, dims):
    return lax.dot_general(a, b, dims, preferred_element_type=F32)


def pieces(x):
    hi = x.astype(BF16)
    lo = (x - hi.astype(F32)).astype(BF16)
    return hi, lo


def pieces3(x):
    hi = x.astype(BF16)
    mid, lo = pieces(x - hi.astype(F32))
    return [hi, mid, lo]


def exact_rows(row, mat, dims):
    stack = jnp.concatenate(pieces3(row), axis=0)
    return jnp.sum(dot(stack, mat, dims), axis=0, keepdims=True)


def send_half(a_ref, b_ref, send_ref, own_ref, sems):
    mine, theirs = halves(send_ref.shape[1])
    pairs = [
        (a_ref.at[theirs], send_ref.at[0]),
        (b_ref.at[theirs], send_ref.at[1]),
        (a_ref.at[mine], own_ref.at[0]),
        (b_ref.at[mine], own_ref.at[1]),
    ]
    copy_all(pairs, sems)


def halves(size):
    core = lax.axis_index("c")
    mine = pl.ds(pl.multiple_of(core * size, 16), size)
    theirs = pl.ds(pl.multiple_of((1 - core) * size, 16), size)
    return mine, theirs


def merge_query(own, far, out, token):
    token[...] = jnp.zeros(token.shape, F32)
    mine, theirs = halves(own.shape[0])
    out[mine] = own[...]
    out[theirs] = far[...]


def merge_pair(own, far, first, second):
    mine, theirs = halves(own.shape[1])
    for i, out in enumerate((first, second)):
        out[mine] = own[i]
        out[theirs] = far[i]


def head_of(own, got, i, h):
    part = slice(h * HD, (h + 1) * HD)
    return jnp.concatenate([own[i, part], got[i, part]], axis=1)


def columns(rows):
    wide = jnp.concatenate([rows, jnp.zeros((HALF, LANES - HD), F32)], axis=1)
    tall = jnp.concatenate([wide, jnp.zeros((8 - HALF, LANES), F32)], axis=0)
    return jnp.transpose(tall)


def spread(row, n):
    return jnp.broadcast_to(row[None], (n, 1, HD))


def sum_of(got, n, first, last):
    total = got[0, first:last]
    for j in range(1, n):
        total = total + got[j, first:last]
    return total


def state_body(n, rows, kv, kv_got, pay, token, whole):
    token[...] = jnp.zeros(token.shape, F32)
    for h in range(HALF):
        key = jnp.maximum(head_of(kv, kv_got, 0, h), 0)
        val = head_of(kv, kv_got, 1, h)
        whole[h * HD : (h + 1) * HD] = dot(key, val, NT)
        norm = dot(jnp.ones((8, key.shape[1]), BF16), key, NT)[:1]
        pay[:, rows + h : rows + h + 1] = spread(norm, n)
    for j in range(n):
        pay[j, :rows] = whole[j * rows : (j + 1) * rows]


def grad_body(n, rows, scale, got, qg, qg_got, pay, norm_ref, inv_ref, whole):
    total = sum_of(got, n, 0, rows + HALF)
    norm_ref[...] = total[rows:]
    for h in range(HALF):
        query = jnp.maximum(head_of(qg, qg_got, 0, h), 0)
        grad = head_of(qg, qg_got, 1, h)
        inv = 1.0 / (exact_rows(total[rows + h : rows + h + 1], query, NN) + EPSILON)
        inv_ref[h : h + 1] = inv
        hi, lo = pieces(grad.astype(F32) * (inv * scale))
        whole[h * HD : (h + 1) * HD] = dot(query, hi, NT) + dot(query, lo, NT)
    shard = total[:rows]
    for j in range(n):
        pay[j, :rows] = shard
        pay[j, rows : 2 * rows] = whole[j * rows : (j + 1) * rows]


def query_body(
    n, rows, scale, got, qg, qg_got, norm_ref, inv_ref, pay, out_mine, out_theirs, whole
):
    total = sum_of(got, n, rows, 2 * rows)
    for j in range(n):
        whole[j * rows : (j + 1) * rows] = got[j, :rows]
        pay[j, :rows] = total
    norms = columns(norm_ref[...])
    tok = out_mine.shape[1]
    for h in range(HALF):
        part = slice(h * HD, (h + 1) * HD)
        feat = jnp.maximum(head_of(qg, qg_got, 0, h), 0)
        query = feat.astype(F32)
        grad = head_of(qg, qg_got, 1, h)
        hi, lo = pieces(whole[part])
        prod = dot(hi, grad, NN) + dot(lo, grad, NN)
        inv = inv_ref[h : h + 1]
        weight = inv * scale
        proj = jnp.sum(query * prod, axis=0, keepdims=True) * weight * inv
        pay[:, rows + h : rows + h + 1] = spread(-exact_rows(proj, feat, NT), n)
        out = prod * weight - norms[:HD, h : h + 1] * proj
        out = jnp.where(query > 0, out, 0.0).astype(BF16)
        out_mine[part] = out[:, :tok]
        out_theirs[part] = out[:, tok:]


def key_body(n, rows, got, kv, kv_got, out_mine, out_theirs, whole):
    for j in range(n):
        whole[j * rows : (j + 1) * rows] = got[j, :rows]
    norms = columns(sum_of(got, n, rows, rows + HALF))
    tok = out_mine.shape[2]
    for h in range(HALF):
        part = slice(h * HD, (h + 1) * HD)
        key = head_of(kv, kv_got, 0, h)
        val = head_of(kv, kv_got, 1, h)
        hi, lo = pieces(whole[part])
        k_out = dot(hi, val, NN) + dot(lo, val, NN) + norms[:HD, h : h + 1]
        k_out = jnp.where(key.astype(F32) > 0, k_out, 0.0).astype(BF16)
        feat = jnp.maximum(key, 0)
        v_out = (dot(hi, feat, TN) + dot(lo, feat, TN)).astype(BF16)
        out_mine[0, part] = k_out[:, :tok]
        out_theirs[0, part] = k_out[:, tok:]
        out_mine[1, part] = v_out[:, :tok]
        out_theirs[1, part] = v_out[:, tok:]


def shift(x, step):
    rows = lax.broadcasted_iota(jnp.int32, x.shape, 0)
    moved = pltpu.roll(x, step % x.shape[0], 0)
    edge = 0 if step > 0 else x.shape[0] - 1
    return jnp.where(rows == edge, 0.0, moved)


def taps(sources, weight, picks, lanes):
    planes = [ref[:, lanes].astype(F32) for ref in sources]

    def column(j):
        return sum(p * weight[i, pl.ds(j, 1), lanes] for p, i in zip(planes, picks))

    return (column(1) + shift(column(0), -1) + shift(column(2), 1)).astype(BF16)


def columns_at(start, width):
    return pl.ds(pl.multiple_of(start, LANES), width)


def halve_body(at, row, weight, send, mine, weight_mine, token, sems):
    token[...] = jnp.zeros(token.shape, F32)
    side = lax.axis_index("x")
    half, width = row.shape[3] // 2, mine.shape[1]
    pairs = [
        row.at[0, 0, :, columns_at((1 - side) * half + at, width)],
        row.at[0, 0, :, columns_at(side * half + at, width)],
        weight.at[:, :, columns_at(side * half + at, width)],
    ]
    copy_all(list(zip(pairs, (send, mine, weight_mine))), sems)


def send_body(mine, got, far, weight, out, token, *held):
    *held, made, sems = held
    token[...] = jnp.zeros(token.shape, F32)
    copy_all(list(zip((mine, got, far, weight), held)), sems)
    mine, got, far, weight = held
    side = lax.axis_index("x")
    width = mine.shape[1]

    @pl.loop(0, width // LANES)
    def _(t):
        lanes = columns_at(t * LANES, LANES)
        made[:, lanes] = taps((got, mine, far), weight, (1, 2 - 2 * side, 2 * side), lanes)

    copy_all([(made, out)], sems)


def keep_body(at, mine, got, far, back, weight, *refs):
    out, token, *held = refs[-9:]
    *held, made, sems = held
    token[...] = jnp.zeros(token.shape, F32)
    copy_all(list(zip((mine, got, far, back, weight), held)), sems)
    mine, got, far, back, weight = held
    side = lax.axis_index("x")
    width = mine.shape[1]

    @pl.loop(0, width // LANES)
    def _(t):
        lanes = columns_at(t * LANES, LANES)
        made[:, lanes] = taps((mine, got, far), weight, (1, 2 * side, 2 - 2 * side), lanes)

    half = out.shape[3] // 2
    here = columns_at(side * half + at, width)
    there = columns_at((1 - side) * half + at, width)
    copy_all([(made, out.at[0, 0, :, here]), (back, out.at[0, 0, :, there])], sems)


def shards(queries, key_proj, value_proj, attn_grad, conv_grad, conv_weight):
    tok = queries.shape[0] * queries.shape[1] * queries.shape[2]
    tokens_all = tok * lax.axis_size(("y", "c", "z", "x"))
    scale = math.sqrt(tokens_all)
    n = lax.axis_size(CHIPS)
    rows = -(-HALF * HD // n)
    pay_one = -(-(rows + HALF) // 8) * 8
    pay_two = -(-2 * rows // 8) * 8
    swap = [(0, 1), (1, 0)]
    sd = jax.ShapeDtypeStruct
    scratch = [pltpu.VMEM((n * rows, HD), F32)]
    half = HALF * HD
    pair_shape = sd((2, half, tok), BF16)
    q, k, v, g = (
        jnp.swapaxes(a, 2, 3).reshape(2 * half, tok)
        for a in (queries, key_proj, value_proj, attn_grad)
    )

    z_size = lax.axis_size("z")
    ahead = [(z, z + 1) for z in range(z_size - 1)]
    even_up = [(2 * i, 2 * j) for i, j in ahead]
    even_down = [(2 * j, 2 * i) for i, j in ahead]
    odd_up = [(2 * i + 1, 2 * j + 1) for i, j in ahead]
    odd_down = [(2 * j + 1, 2 * i + 1) for i, j in ahead]
    cols, ch = conv_grad.shape[2:]
    tiles = ch // (2 * LANES)
    cuts = [tiles * part // 22 for part in CUTS] + [tiles]
    starts = [LANES * c for c in cuts[:-1]]
    widths = [LANES * (d - c) for c, d in zip(cuts, cuts[1:])]
    token = sd((8, LANES), F32)

    def hold(i, count):
        return [pltpu.VMEM((cols, widths[i]), BF16)] * count

    def hold_weight(i):
        return [pltpu.VMEM((3, 3, widths[i]), F32)]

    def sems(count):
        return [pltpu.SemaphoreType.DMA((count,))]

    def halve(i, after):
        return call(
            functools.partial(halve_body, starts[i]),
            [sd((cols, widths[i]), BF16)] * 2 + [sd((3, 3, widths[i]), F32), token],
            (held_in_hbm(conv_grad), held_in_hbm(conv_weight)),
            sems(3),
            after=after,
            any_in=True,
        )

    def move_in(i):
        near = lax.ppermute(row_send[i], "x", swap)
        return held_in_hbm(near), held_in_hbm(lax.ppermute(row_mine[i], ("z", "x"), even_down + odd_up))

    def send_out(i):
        return call(
            send_body,
            [sd((cols, widths[i]), BF16), token],
            (row_mine[i], near[i], far[i], weight[i]),
            hold(i, 3) + hold_weight(i) + hold(i, 1) + sems(4),
            flops=20 * cols * widths[i],
            any_in=True,
            hbm_out=1,
        )

    def finish(i, before=()):
        return call(
            functools.partial(keep_body, starts[i]),
            [sd(conv_grad.shape, BF16), token],
            (row_mine[i], near[i], onward[i], back[i], weight[i], *before),
            hold(i, 4) + hold_weight(i) + hold(i, 1) + sems(5),
            flops=20 * cols * widths[i],
            any_in=True,
            hbm_out=1,
            alias={5: 0} if before else None,
        )

    row_mine, row_send, weight, halved, near, far = {}, {}, {}, {}, {}, {}
    sent, onward, back, kept = {}, {}, {}, {}
    for i in range(CHUNKS):
        row_send[i], row_mine[i], weight[i], halved[i] = halve(i, ())
        near[i], far[i] = move_in(i)
        onward[i] = lax.ppermute(near[i], ("z", "x"), even_up + odd_down)
        out_send, sent[i] = send_out(i)
        back[i] = lax.ppermute(out_send, "x", swap)
        input_grad, kept[i] = finish(i, (input_grad,) if i else ())
    def part(first, second, after=()):
        return call(
            send_half,
            [pair_shape] * 2,
            (held_in_hbm(first), held_in_hbm(second)),
            sems(4),
            after=after,
            any_in=True,
        )

    kv_send, kv = part(k, v, (halved[0],))
    kv_got = lax.ppermute(kv_send, "c", swap)
    qg_send, qg = part(q, g)
    qg_got = lax.ppermute(qg_send, "c", swap)

    def exchange(pay):
        return lax.all_to_all(pay, CHIPS, split_axis=0, concat_axis=0, tiled=True)

    macs = HALF * 2 * tok * HD * HD
    pay, started = call(
        functools.partial(state_body, n, rows),
        [sd((n, pay_one, HD), F32), token],
        (kv, kv_got),
        scratch,
        flops=2 * macs,
        pinned=True,
    )
    got = exchange(pay)
    ties = {"near": near, "far": far, "sent": sent, "kept": kept, "halved": halved}

    def tied(stage):
        return tuple(ties[name][i] for name, i in ORDER[stage])

    pay, norm, inv = call(
        functools.partial(grad_body, n, rows, scale),
        [sd((n, pay_two, HD), F32), sd((HALF, HD), F32), sd((HALF, 2 * tok), F32)],
        (got, qg, qg_got),
        scratch,
        flops=4 * macs,
        pinned=True,
        after=tied(0),
    )
    got = exchange(pay)
    pay, query_mine, query_send = call(
        functools.partial(query_body, n, rows, scale),
        [sd((n, pay_one, HD), F32)] + [sd((half, tok), BF16)] * 2,
        (got, qg, qg_got, norm, inv),
        scratch,
        flops=4 * macs,
        pinned=True,
        after=tied(1),
    )
    query_got = lax.ppermute(query_send, "c", swap)
    whole_shape = sd((2 * half, tok), BF16)
    query_out, merged = call(merge_query, [whole_shape, token], (query_mine, query_got))
    got = exchange(pay)
    key_mine, key_send = call(
        functools.partial(key_body, n, rows),
        [pair_shape] * 2,
        (got, kv, kv_got),
        scratch,
        flops=8 * macs,
        after=(merged, *tied(2)),
    )
    key_got = lax.ppermute(key_send, "c", swap)
    outs = query_out, *call(merge_pair, [whole_shape] * 2, (key_mine, key_got))
    outs = [jnp.swapaxes(o.reshape(*queries.shape[:2], 2 * half, -1), 2, 3) for o in outs]
    return (*outs, input_grad)


def solution(mesh):
    frames, bands = mesh.shape["frame"], mesh.shape["row"]
    fine = Mesh(mesh.devices.reshape(frames // 2, 2, bands // 2, 2), ("y", "c", "z", "x"))
    split = P(("y", "c"), ("z", "x"), None, None)
    return jax.shard_map(
        shards,
        mesh=fine,
        in_specs=(split,) * 5 + (P(),),
        out_specs=(split,) * 4,
        check_vma=False,
    )
```

```python
import functools
import math

import jax
import jax.numpy as jnp
from jax import lax
from jax.experimental import pallas as pl
from jax.experimental.pallas import tpu as pltpu
from jax.sharding import Mesh, PartitionSpec as P

HEADS = 10
HD = 112
EPSILON = 1e-06
HALF = HEADS // 2
LANES = 128
CUTS = (0,)
CHUNKS = 1
EARLY = 1
ORDER = [[], [('sent', 0)], [('kept', 0)]]
SEND_COST = 500000000
KEEP_COST = 10000000000
CHIPS = ("y", "z", "x")
F32 = jnp.float32
BF16 = jnp.bfloat16

NT = (((1,), (1,)), ((), ()))
TN = (((0,), (0,)), ((), ()))
NN = (((1,), (0,)), ((), ()))


def held_in_hbm(x):
    return pltpu.with_memory_space_constraint(x, pltpu.HBM)


def call(body, outs, args, scratch=(), flops=0, after=(), any_in=False, hbm_out=0, pinned=False, alias=None):
    size = sum(math.prod(a.shape) * a.dtype.itemsize for a in list(args) + list(outs))
    fast = pl.BlockSpec(memory_space=pltpu.VMEM)
    slow = pl.BlockSpec(memory_space=pltpu.HBM)
    free = pl.BlockSpec(memory_space=pl.ANY)
    scratch = list(scratch)
    if pinned:
        scratch += [pltpu.VMEM(outs[0].shape, outs[0].dtype), pltpu.SemaphoreType.DMA((1,))]

    def ordered(*refs):
        ins = refs[: len(args)]
        made = refs[len(args) + len(after) :][: len(outs)]
        held = refs[len(args) + len(after) + len(outs) :]
        if not pinned:
            body(*ins, *made, *held)
            return
        first, sem = held[-2:]
        body(*ins, first, *made[1:], *held[:-2])
        copy_all([(first, made[0])], sem)

    out_specs = [slow if i < max(hbm_out, pinned) else fast for i in range(len(outs))]
    shapes = [
        pltpu.HBM(o.shape, o.dtype) if i < max(hbm_out, pinned) else o
        for i, o in enumerate(outs)
    ]
    return pl.pallas_call(
        ordered,
        out_shape=shapes,
        in_specs=[free if any_in else fast] * len(args) + [free] * len(after),
        out_specs=out_specs,
        scratch_shapes=scratch,
        compiler_params=pltpu.CompilerParams(vmem_limit_bytes=16 * 1024 * 1024),
        cost_estimate=pl.CostEstimate(flops=flops, bytes_accessed=size, transcendentals=0),
        input_output_aliases=alias or {},
    )(*args, *after)


def copy_all(pairs, sems):
    copies = [pltpu.make_async_copy(a, b, sems.at[i]) for i, (a, b) in enumerate(pairs)]
    for c in copies:
        c.start()
    for c in copies:
        c.wait()


def dot(a, b, dims):
    return lax.dot_general(a, b, dims, preferred_element_type=F32)


def pieces(x):
    hi = x.astype(BF16)
    lo = (x - hi.astype(F32)).astype(BF16)
    return hi, lo


def pieces3(x):
    hi = x.astype(BF16)
    mid, lo = pieces(x - hi.astype(F32))
    return [hi, mid, lo]


def exact_rows(row, mat, dims):
    stack = jnp.concatenate(pieces3(row), axis=0)
    return jnp.sum(dot(stack, mat, dims), axis=0, keepdims=True)


def send_half(a_ref, b_ref, send_ref, own_ref, sems):
    mine, theirs = halves(send_ref.shape[1])
    pairs = [
        (a_ref.at[theirs], send_ref.at[0]),
        (b_ref.at[theirs], send_ref.at[1]),
        (a_ref.at[mine], own_ref.at[0]),
        (b_ref.at[mine], own_ref.at[1]),
    ]
    copy_all(pairs, sems)


def first_body(row, weight, a_ref, b_ref, send, mine, weight_mine, token, kv_send, kv, sems):
    token[...] = jnp.zeros(token.shape, F32)
    side = lax.axis_index("x")
    own, theirs = halves(kv_send.shape[1])
    half = row.shape[3] // 2
    pairs = [
        (a_ref.at[theirs], kv_send.at[0]),
        (b_ref.at[theirs], kv_send.at[1]),
        (a_ref.at[own], kv.at[0]),
        (b_ref.at[own], kv.at[1]),
        (row.at[0, 0, :, columns_at(side * half, half)], mine),
        (row.at[0, 0, :, columns_at((1 - side) * half, half)], send),
        (weight.at[:, :, columns_at(side * half, half)], weight_mine),
    ]
    copy_all(pairs, sems)


def halves(size):
    core = lax.axis_index("c")
    mine = pl.ds(pl.multiple_of(core * size, 16), size)
    theirs = pl.ds(pl.multiple_of((1 - core) * size, 16), size)
    return mine, theirs


def merge_query(own, far, out, token):
    token[...] = jnp.zeros(token.shape, F32)
    mine, theirs = halves(own.shape[0])
    out[mine] = own[...]
    out[theirs] = far[...]


def merge_pair(own, far, first, second):
    mine, theirs = halves(own.shape[1])
    for i, out in enumerate((first, second)):
        out[mine] = own[i]
        out[theirs] = far[i]


def head_of(own, got, i, h):
    part = slice(h * HD, (h + 1) * HD)
    return jnp.concatenate([own[i, part], got[i, part]], axis=1)


def columns(rows):
    wide = jnp.concatenate([rows, jnp.zeros((HALF, LANES - HD), F32)], axis=1)
    tall = jnp.concatenate([wide, jnp.zeros((8 - HALF, LANES), F32)], axis=0)
    return jnp.transpose(tall)


def spread(row, n):
    return jnp.broadcast_to(row[None], (n, 1, HD))


def sum_of(got, n, first, last):
    total = got[0, first:last]
    for j in range(1, n):
        total = total + got[j, first:last]
    return total


def state_body(n, rows, kv, kv_got, pay, token, whole):
    token[...] = jnp.zeros(token.shape, F32)
    for h in range(HALF):
        key = jnp.maximum(head_of(kv, kv_got, 0, h), 0)
        val = head_of(kv, kv_got, 1, h)
        whole[h * HD : (h + 1) * HD] = dot(key, val, NT)
        norm = dot(jnp.ones((8, key.shape[1]), BF16), key, NT)[:1]
        pay[:, rows + h : rows + h + 1] = spread(norm, n)
    for j in range(n):
        pay[j, :rows] = whole[j * rows : (j + 1) * rows]


def grad_body(n, rows, scale, got, qg, qg_got, pay, norm_ref, inv_ref, whole):
    total = sum_of(got, n, 0, rows + HALF)
    norm_ref[...] = total[rows:]
    for h in range(HALF):
        query = jnp.maximum(head_of(qg, qg_got, 0, h), 0)
        grad = head_of(qg, qg_got, 1, h)
        inv = 1.0 / (exact_rows(total[rows + h : rows + h + 1], query, NN) + EPSILON)
        inv_ref[h : h + 1] = inv
        hi, lo = pieces(grad.astype(F32) * (inv * scale))
        whole[h * HD : (h + 1) * HD] = dot(query, hi, NT) + dot(query, lo, NT)
    shard = total[:rows]
    for j in range(n):
        pay[j, :rows] = shard
        pay[j, rows : 2 * rows] = whole[j * rows : (j + 1) * rows]


def query_body(
    n, rows, scale, got, qg, qg_got, norm_ref, inv_ref, pay, out_mine, out_theirs, whole
):
    total = sum_of(got, n, rows, 2 * rows)
    for j in range(n):
        whole[j * rows : (j + 1) * rows] = got[j, :rows]
        pay[j, :rows] = total
    norms = columns(norm_ref[...])
    tok = out_mine.shape[1]
    for h in range(HALF):
        part = slice(h * HD, (h + 1) * HD)
        feat = jnp.maximum(head_of(qg, qg_got, 0, h), 0)
        query = feat.astype(F32)
        grad = head_of(qg, qg_got, 1, h)
        hi, lo = pieces(whole[part])
        prod = dot(hi, grad, NN) + dot(lo, grad, NN)
        inv = inv_ref[h : h + 1]
        weight = inv * scale
        proj = jnp.sum(query * prod, axis=0, keepdims=True) * weight * inv
        pay[:, rows + h : rows + h + 1] = spread(-exact_rows(proj, feat, NT), n)
        out = prod * weight - norms[:HD, h : h + 1] * proj
        out = jnp.where(query > 0, out, 0.0).astype(BF16)
        out_mine[part] = out[:, :tok]
        out_theirs[part] = out[:, tok:]


def key_body(n, rows, got, kv, kv_got, out_mine, out_theirs, whole):
    for j in range(n):
        whole[j * rows : (j + 1) * rows] = got[j, :rows]
    norms = columns(sum_of(got, n, rows, rows + HALF))
    tok = out_mine.shape[2]
    for h in range(HALF):
        part = slice(h * HD, (h + 1) * HD)
        key = head_of(kv, kv_got, 0, h)
        val = head_of(kv, kv_got, 1, h)
        hi, lo = pieces(whole[part])
        k_out = dot(hi, val, NN) + dot(lo, val, NN) + norms[:HD, h : h + 1]
        k_out = jnp.where(key.astype(F32) > 0, k_out, 0.0).astype(BF16)
        feat = jnp.maximum(key, 0)
        v_out = (dot(hi, feat, TN) + dot(lo, feat, TN)).astype(BF16)
        out_mine[0, part] = k_out[:, :tok]
        out_theirs[0, part] = k_out[:, tok:]
        out_mine[1, part] = v_out[:, :tok]
        out_theirs[1, part] = v_out[:, tok:]


def shift(x, step):
    rows = lax.broadcasted_iota(jnp.int32, x.shape, 0)
    moved = pltpu.roll(x, step % x.shape[0], 0)
    edge = 0 if step > 0 else x.shape[0] - 1
    return jnp.where(rows == edge, 0.0, moved)


def taps(sources, weight, picks, lanes):
    planes = [ref[:, lanes].astype(F32) for ref in sources]

    def column(j):
        return sum(p * weight[i, pl.ds(j, 1), lanes] for p, i in zip(planes, picks))

    return (column(1) + shift(column(0), -1) + shift(column(2), 1)).astype(BF16)


def columns_at(start, width):
    return pl.ds(pl.multiple_of(start, LANES), width)


def halve_body(at, row, weight, send, mine, weight_mine, token, sems):
    token[...] = jnp.zeros(token.shape, F32)
    side = lax.axis_index("x")
    half, width = row.shape[3] // 2, mine.shape[1]
    pairs = [
        row.at[0, 0, :, columns_at((1 - side) * half + at, width)],
        row.at[0, 0, :, columns_at(side * half + at, width)],
        weight.at[:, :, columns_at(side * half + at, width)],
    ]
    copy_all(list(zip(pairs, (send, mine, weight_mine))), sems)


def send_body(mine, got, far, weight, out, token, *held):
    *held, made, sems = held
    token[...] = jnp.zeros(token.shape, F32)
    copy_all(list(zip((mine, got, far, weight), held)), sems)
    mine, got, far, weight = held
    side = lax.axis_index("x")
    width = mine.shape[1]

    @pl.loop(0, width // LANES)
    def _(t):
        lanes = columns_at(t * LANES, LANES)
        made[:, lanes] = taps((got, mine, far), weight, (1, 2 - 2 * side, 2 * side), lanes)

    copy_all([(made, out)], sems)


def keep_body(at, mine, got, far, back, weight, *refs):
    out, token, *held = refs[-9:]
    *held, made, sems = held
    token[...] = jnp.zeros(token.shape, F32)
    copy_all(list(zip((mine, got, far, back, weight), held)), sems)
    mine, got, far, back, weight = held
    side = lax.axis_index("x")
    width = mine.shape[1]

    @pl.loop(0, width // LANES)
    def _(t):
        lanes = columns_at(t * LANES, LANES)
        made[:, lanes] = taps((mine, got, far), weight, (1, 2 * side, 2 - 2 * side), lanes)

    half = out.shape[3] // 2
    here = columns_at(side * half + at, width)
    there = columns_at((1 - side) * half + at, width)
    copy_all([(made, out.at[0, 0, :, here]), (back, out.at[0, 0, :, there])], sems)


def shards(queries, key_proj, value_proj, attn_grad, conv_grad, conv_weight):
    tok = queries.shape[0] * queries.shape[1] * queries.shape[2]
    tokens_all = tok * lax.axis_size(("y", "c", "z", "x"))
    scale = math.sqrt(tokens_all)
    n = lax.axis_size(CHIPS)
    rows = -(-HALF * HD // n)
    pay_one = -(-(rows + HALF) // 8) * 8
    pay_two = -(-2 * rows // 8) * 8
    swap = [(0, 1), (1, 0)]
    sd = jax.ShapeDtypeStruct
    scratch = [pltpu.VMEM((n * rows, HD), F32)]
    half = HALF * HD
    pair_shape = sd((2, half, tok), BF16)
    q, k, v, g = (
        jnp.swapaxes(a, 2, 3).reshape(2 * half, tok)
        for a in (queries, key_proj, value_proj, attn_grad)
    )

    z_size = lax.axis_size("z")
    ahead = [(z, z + 1) for z in range(z_size - 1)]
    even_up = [(2 * i, 2 * j) for i, j in ahead]
    even_down = [(2 * j, 2 * i) for i, j in ahead]
    odd_up = [(2 * i + 1, 2 * j + 1) for i, j in ahead]
    odd_down = [(2 * j + 1, 2 * i + 1) for i, j in ahead]
    cols, ch = conv_grad.shape[2:]
    tiles = ch // (2 * LANES)
    cuts = [tiles * part // 22 for part in CUTS] + [tiles]
    starts = [LANES * c for c in cuts[:-1]]
    widths = [LANES * (d - c) for c, d in zip(cuts, cuts[1:])]
    token = sd((8, LANES), F32)

    def hold(i, count):
        return [pltpu.VMEM((cols, widths[i]), BF16)] * count

    def hold_weight(i):
        return [pltpu.VMEM((3, 3, widths[i]), F32)]

    def sems(count):
        return [pltpu.SemaphoreType.DMA((count,))]

    def halve(i, after):
        return call(
            functools.partial(halve_body, starts[i]),
            [sd((cols, widths[i]), BF16)] * 2 + [sd((3, 3, widths[i]), F32), token],
            (held_in_hbm(conv_grad), held_in_hbm(conv_weight)),
            sems(3),
            after=after,
            any_in=True,
        )

    def move_in(i):
        near = lax.ppermute(row_send[i], "x", swap)
        return held_in_hbm(near), held_in_hbm(lax.ppermute(row_mine[i], ("z", "x"), even_down + odd_up))

    def send_out(i):
        return call(
            send_body,
            [sd((cols, widths[i]), BF16), token],
            (row_mine[i], near[i], far[i], weight[i]),
            hold(i, 3) + hold_weight(i) + hold(i, 1) + sems(4),
            flops=SEND_COST,
            any_in=True,
            hbm_out=1,
        )

    def finish(i, before=()):
        return call(
            functools.partial(keep_body, starts[i]),
            [sd(conv_grad.shape, BF16), token],
            (row_mine[i], near[i], onward[i], back[i], weight[i], *before),
            hold(i, 4) + hold_weight(i) + hold(i, 1) + sems(5),
            flops=KEEP_COST,
            any_in=True,
            hbm_out=1,
            alias={5: 0} if before else None,
        )

    row_mine, row_send, weight, halved, near, far = {}, {}, {}, {}, {}, {}
    sent, onward, back, kept = {}, {}, {}, {}
    for i in range(CHUNKS):
        row_send[i], row_mine[i], weight[i], halved[i], kv_send, kv = call(
            first_body,
            [sd((cols, widths[i]), BF16)] * 2
            + [sd((3, 3, widths[i]), F32), token, pair_shape, pair_shape],
            tuple(map(held_in_hbm, (conv_grad, conv_weight, k, v))),
            sems(7),
            any_in=True,
        )
        near[i], far[i] = move_in(i)
        onward[i] = lax.ppermute(near[i], ("z", "x"), even_up + odd_down)
        out_send, sent[i] = send_out(i)
        back[i] = lax.ppermute(out_send, "x", swap)
        input_grad, kept[i] = finish(i, (input_grad,) if i else ())
    def part(first, second, after=()):
        return call(
            send_half,
            [pair_shape] * 2,
            (held_in_hbm(first), held_in_hbm(second)),
            sems(4),
            after=after,
            any_in=True,
        )

    kv_got = lax.ppermute(kv_send, "c", swap)
    qg_send, qg = part(q, g)
    qg_got = lax.ppermute(qg_send, "c", swap)

    def exchange(pay):
        return lax.all_to_all(pay, CHIPS, split_axis=0, concat_axis=0, tiled=True)

    macs = HALF * 2 * tok * HD * HD
    pay, started = call(
        functools.partial(state_body, n, rows),
        [sd((n, pay_one, HD), F32), token],
        (kv, kv_got),
        scratch,
        flops=2 * macs,
        pinned=True,
    )
    got = exchange(pay)
    ties = {"near": near, "far": far, "sent": sent, "kept": kept, "halved": halved}

    def tied(stage):
        return tuple(ties[name][i] for name, i in ORDER[stage])

    pay, norm, inv = call(
        functools.partial(grad_body, n, rows, scale),
        [sd((n, pay_two, HD), F32), sd((HALF, HD), F32), sd((HALF, 2 * tok), F32)],
        (got, qg, qg_got),
        scratch,
        flops=4 * macs,
        pinned=True,
        after=tied(0),
    )
    got = exchange(pay)
    pay, query_mine, query_send = call(
        functools.partial(query_body, n, rows, scale),
        [sd((n, pay_one, HD), F32)] + [sd((half, tok), BF16)] * 2,
        (got, qg, qg_got, norm, inv),
        scratch,
        flops=4 * macs,
        pinned=True,
        after=tied(1),
    )
    query_got = lax.ppermute(query_send, "c", swap)
    whole_shape = sd((2 * half, tok), BF16)
    query_out, merged = call(merge_query, [whole_shape, token], (query_mine, query_got))
    got = exchange(pay)
    key_mine, key_send = call(
        functools.partial(key_body, n, rows),
        [pair_shape] * 2,
        (got, kv, kv_got),
        scratch,
        flops=8 * macs,
        after=(merged, *tied(2)),
    )
    key_got = lax.ppermute(key_send, "c", swap)
    outs = query_out, *call(merge_pair, [whole_shape] * 2, (key_mine, key_got))
    outs = [jnp.swapaxes(o.reshape(*queries.shape[:2], 2 * half, -1), 2, 3) for o in outs]
    return (*outs, input_grad)


def solution(mesh):
    frames, bands = mesh.shape["frame"], mesh.shape["row"]
    fine = Mesh(mesh.devices.reshape(frames // 2, 2, bands // 2, 2), ("y", "c", "z", "x"))
    split = P(("y", "c"), ("z", "x"), None, None)
    return jax.shard_map(
        shards,
        mesh=fine,
        in_specs=(split,) * 5 + (P(),),
        out_specs=(split,) * 4,
        check_vma=False,
    )
```

```python
import functools
import math

import jax
import jax.numpy as jnp
from jax import lax
from jax.experimental import pallas as pl
from jax.experimental.pallas import tpu as pltpu
from jax.sharding import Mesh, PartitionSpec as P

HEADS = 10
HD = 112
EPSILON = 1e-06
HALF = HEADS // 2
LANES = 128
PIECES = 4
CUTS = (0,)
CHUNKS = 1
EARLY = 1
ORDER = [[], [('sent', 0)], [('kept', 0)]]
SEND_COST = 500000000
KEEP_COST = 10000000000
CHIPS = ("y", "z", "x")
F32 = jnp.float32
BF16 = jnp.bfloat16

NT = (((1,), (1,)), ((), ()))
TN = (((0,), (0,)), ((), ()))
NN = (((1,), (0,)), ((), ()))


def held_in_hbm(x):
    return pltpu.with_memory_space_constraint(x, pltpu.HBM)


def call(body, outs, args, scratch=(), flops=0, after=(), any_in=False, hbm_out=0, pinned=0, alias=None):
    size = sum(math.prod(a.shape) * a.dtype.itemsize for a in list(args) + list(outs))
    fast = pl.BlockSpec(memory_space=pltpu.VMEM)
    slow = pl.BlockSpec(memory_space=pltpu.HBM)
    free = pl.BlockSpec(memory_space=pl.ANY)
    scratch = list(scratch)
    if pinned:
        scratch += [pltpu.VMEM(o.shape, o.dtype) for o in outs[:pinned]]
        scratch += [pltpu.SemaphoreType.DMA((pinned,))]

    def ordered(*refs):
        ins = refs[: len(args)]
        made = refs[len(args) + len(after) :][: len(outs)]
        held = refs[len(args) + len(after) + len(outs) :]
        if not pinned:
            body(*ins, *made, *held)
            return
        *held, sem = held
        kept, held = held[-pinned:], held[:-pinned]
        body(*ins, *kept, *made[pinned:], *held)
        copy_all(list(zip(kept, made)), sem)

    out_specs = [slow if i < max(hbm_out, pinned) else fast for i in range(len(outs))]
    shapes = [
        pltpu.HBM(o.shape, o.dtype) if i < max(hbm_out, pinned) else o
        for i, o in enumerate(outs)
    ]
    return pl.pallas_call(
        ordered,
        out_shape=shapes,
        in_specs=[free if any_in else fast] * len(args) + [free] * len(after),
        out_specs=out_specs,
        scratch_shapes=scratch,
        compiler_params=pltpu.CompilerParams(vmem_limit_bytes=16 * 1024 * 1024),
        cost_estimate=pl.CostEstimate(flops=flops, bytes_accessed=size, transcendentals=0),
        input_output_aliases=alias or {},
    )(*args, *after)


def copy_all(pairs, sems):
    copies = [pltpu.make_async_copy(a, b, sems.at[i]) for i, (a, b) in enumerate(pairs)]
    for c in copies:
        c.start()
    for c in copies:
        c.wait()


def dot(a, b, dims):
    return lax.dot_general(a, b, dims, preferred_element_type=F32)


def pieces(x):
    hi = x.astype(BF16)
    lo = (x - hi.astype(F32)).astype(BF16)
    return hi, lo


def pieces3(x):
    hi = x.astype(BF16)
    mid, lo = pieces(x - hi.astype(F32))
    return [hi, mid, lo]


def exact_rows(row, mat, dims):
    stack = jnp.concatenate(pieces3(row), axis=0)
    return jnp.sum(dot(stack, mat, dims), axis=0, keepdims=True)


def send_half(a_ref, b_ref, send_ref, own_ref, sems):
    mine, theirs = halves(send_ref.shape[1])
    pairs = [
        (a_ref.at[theirs], send_ref.at[0]),
        (b_ref.at[theirs], send_ref.at[1]),
        (a_ref.at[mine], own_ref.at[0]),
        (b_ref.at[mine], own_ref.at[1]),
    ]
    copy_all(pairs, sems)


def first_body(row, weight, send, mine, weight_mine, token, sems):
    token[...] = jnp.zeros(token.shape, F32)
    side = lax.axis_index("x")
    half = mine.shape[1]
    own = columns_at(side * half, half)
    other = columns_at((1 - side) * half, half)
    pairs = [
        (row.at[0, 0, :, own], mine),
        (row.at[0, 0, :, other], send),
        (weight.at[:, :, own], weight_mine),
    ]
    copy_all(pairs, sems)


def halves(size):
    core = lax.axis_index("c")
    mine = pl.ds(pl.multiple_of(core * size, 16), size)
    theirs = pl.ds(pl.multiple_of((1 - core) * size, 16), size)
    return mine, theirs


def merge_query(own, far, out, token):
    token[...] = jnp.zeros(token.shape, F32)
    mine, theirs = halves(own.shape[0])
    out[mine] = own[...]
    out[theirs] = far[...]


def place_own(own, first, second, sems):
    mine, _ = halves(own.shape[1])
    copy_all([(own.at[0], first.at[mine]), (own.at[1], second.at[mine])], sems)


def place_far(far, first_in, second_in, first, second, sems):
    _, theirs = halves(far.shape[1])
    copy_all([(far.at[0], first.at[theirs]), (far.at[1], second.at[theirs])], sems)


def head_of(own, got, i, h):
    part = slice(h * HD, (h + 1) * HD)
    return jnp.concatenate([own[i, part], got[i, part]], axis=1)


def columns(rows):
    wide = jnp.concatenate([rows, jnp.zeros((HALF, LANES - HD), F32)], axis=1)
    tall = jnp.concatenate([wide, jnp.zeros((8 - HALF, LANES), F32)], axis=0)
    return jnp.transpose(tall)


def spread(row, n):
    return jnp.broadcast_to(row[None], (n, 1, HD))


def sum_of(got, n, first, last):
    total = got[0, first:last]
    for j in range(1, n):
        total = total + got[j, first:last]
    return total


def state_body(n, rows, kv, kv_got, pay, token, whole):
    token[...] = jnp.zeros(token.shape, F32)
    for h in range(HALF):
        key = jnp.maximum(head_of(kv, kv_got, 0, h), 0)
        val = head_of(kv, kv_got, 1, h)
        whole[h * HD : (h + 1) * HD] = dot(key, val, NT)
        norm = dot(jnp.ones((8, key.shape[1]), BF16), key, NT)[:1]
        pay[:, rows + h : rows + h + 1] = spread(norm, n)
    for j in range(n):
        pay[j, :rows] = whole[j * rows : (j + 1) * rows]


def grad_body(n, rows, scale, got, qg, qg_got, pay, norm_ref, inv_ref, whole):
    total = sum_of(got, n, 0, rows + HALF)
    norm_ref[...] = total[rows:]
    for h in range(HALF):
        query = jnp.maximum(head_of(qg, qg_got, 0, h), 0)
        grad = head_of(qg, qg_got, 1, h)
        inv = 1.0 / (exact_rows(total[rows + h : rows + h + 1], query, NN) + EPSILON)
        inv_ref[h : h + 1] = inv
        hi, lo = pieces(grad.astype(F32) * (inv * scale))
        whole[h * HD : (h + 1) * HD] = dot(query, hi, NT) + dot(query, lo, NT)
    shard = total[:rows]
    for j in range(n):
        pay[j, :rows] = shard
        pay[j, rows : 2 * rows] = whole[j * rows : (j + 1) * rows]


def query_body(
    n, rows, scale, got, qg, qg_got, norm_ref, inv_ref, pay, out_mine, out_theirs, whole
):
    total = sum_of(got, n, rows, 2 * rows)
    for j in range(n):
        whole[j * rows : (j + 1) * rows] = got[j, :rows]
        pay[j, :rows] = total
    norms = columns(norm_ref[...])
    tok = out_mine.shape[1]
    for h in range(HALF):
        part = slice(h * HD, (h + 1) * HD)
        feat = jnp.maximum(head_of(qg, qg_got, 0, h), 0)
        query = feat.astype(F32)
        grad = head_of(qg, qg_got, 1, h)
        hi, lo = pieces(whole[part])
        prod = dot(hi, grad, NN) + dot(lo, grad, NN)
        inv = inv_ref[h : h + 1]
        weight = inv * scale
        proj = jnp.sum(query * prod, axis=0, keepdims=True) * weight * inv
        pay[:, rows + h : rows + h + 1] = spread(-exact_rows(proj, feat, NT), n)
        out = prod * weight - norms[:HD, h : h + 1] * proj
        out = jnp.where(query > 0, out, 0.0).astype(BF16)
        out_mine[part] = out[:, :tok]
        out_theirs[part] = out[:, tok:]


def key_body(n, rows, got, kv, kv_got, out_mine, out_theirs, whole):
    for j in range(n):
        whole[j * rows : (j + 1) * rows] = got[j, :rows]
    norms = columns(sum_of(got, n, rows, rows + HALF))
    tok = out_mine.shape[2]
    for h in range(HALF):
        part = slice(h * HD, (h + 1) * HD)
        key = head_of(kv, kv_got, 0, h)
        val = head_of(kv, kv_got, 1, h)
        hi, lo = pieces(whole[part])
        k_out = dot(hi, val, NN) + dot(lo, val, NN) + norms[:HD, h : h + 1]
        k_out = jnp.where(key.astype(F32) > 0, k_out, 0.0).astype(BF16)
        feat = jnp.maximum(key, 0)
        v_out = (dot(hi, feat, TN) + dot(lo, feat, TN)).astype(BF16)
        out_mine[0, part] = k_out[:, :tok]
        out_theirs[0, part] = k_out[:, tok:]
        out_mine[1, part] = v_out[:, :tok]
        out_theirs[1, part] = v_out[:, tok:]


def shift(x, step):
    rows = lax.broadcasted_iota(jnp.int32, x.shape, 0)
    moved = pltpu.roll(x, step % x.shape[0], 0)
    edge = 0 if step > 0 else x.shape[0] - 1
    return jnp.where(rows == edge, 0.0, moved)


def taps(sources, weight, picks, lanes):
    planes = [ref[:, lanes].astype(F32) for ref in sources]

    def column(j):
        return sum(p * weight[i, pl.ds(j, 1), lanes] for p, i in zip(planes, picks))

    return (column(1) + shift(column(0), -1) + shift(column(2), 1)).astype(BF16)


def columns_at(start, width):
    return pl.ds(pl.multiple_of(start, LANES), width)


def halve_body(at, row, weight, send, mine, weight_mine, token, sems):
    token[...] = jnp.zeros(token.shape, F32)
    side = lax.axis_index("x")
    half, width = row.shape[3] // 2, mine.shape[1]
    pairs = [
        row.at[0, 0, :, columns_at((1 - side) * half + at, width)],
        row.at[0, 0, :, columns_at(side * half + at, width)],
        weight.at[:, :, columns_at(side * half + at, width)],
    ]
    copy_all(list(zip(pairs, (send, mine, weight_mine))), sems)


def pieces_of(width):
    step = -(-(width // LANES) // PIECES) * LANES
    return [(at, min(step, width - at)) for at in range(0, width, step)]


def staged(sources, held, sems, made, picks, out_of):
    width = made.shape[1]
    loads, stores = [], []
    for n, (at, size) in enumerate(pieces_of(width)):
        part = pl.ds(at, size)
        group = []
        for m, (a, b) in enumerate(zip(sources, held)):
            index = (slice(None),) * (len(a.shape) - 1) + (part,)
            group.append(pltpu.make_async_copy(a.at[index], b.at[index], sems.at[n, m]))
        for c in group:
            c.start()
        loads.append(group)
    *planes, weight = held[:4]
    for n, (at, size) in enumerate(pieces_of(width)):
        for c in loads[n]:
            c.wait()

        @pl.loop(at // LANES, (at + size) // LANES)
        def _(t):
            lanes = columns_at(t * LANES, LANES)
            made[:, lanes] = taps(planes, weight, picks, lanes)

        for m, (a, b) in enumerate(out_of(at, size)):
            c = pltpu.make_async_copy(a, b, sems.at[n, len(sources) + m])
            c.start()
            stores.append(c)
    for c in stores:
        c.wait()


def send_body(mine, got, far, weight, out, token, *held):
    *held, made, sems = held
    token[...] = jnp.zeros(token.shape, F32)
    side = lax.axis_index("x")

    def out_of(at, size):
        return [(made.at[:, pl.ds(at, size)], out.at[:, pl.ds(at, size)])]

    staged((got, mine, far, weight), held, sems, made, (1, 2 - 2 * side, 2 * side), out_of)


def keep_body(mine, got, far, back, weight, out, token, *held):
    *held, made, sems = held
    token[...] = jnp.zeros(token.shape, F32)
    side = lax.axis_index("x")
    half = out.shape[3] // 2

    def out_of(at, size):
        here = columns_at(side * half + at, size)
        there = columns_at((1 - side) * half + at, size)
        part = pl.ds(at, size)
        back_held = held[4]
        return [
            (made.at[:, part], out.at[0, 0, :, here]),
            (back_held.at[:, part], out.at[0, 0, :, there]),
        ]

    sources = (mine, got, far, weight, back)
    staged(sources, held, sems, made, (1, 2 * side, 2 - 2 * side), out_of)


def shards(queries, key_proj, value_proj, attn_grad, conv_grad, conv_weight):
    tok = queries.shape[0] * queries.shape[1] * queries.shape[2]
    tokens_all = tok * lax.axis_size(("y", "c", "z", "x"))
    scale = math.sqrt(tokens_all)
    n = lax.axis_size(CHIPS)
    rows = -(-HALF * HD // n)
    pay_one = -(-(rows + HALF) // 8) * 8
    pay_two = -(-2 * rows // 8) * 8
    swap = [(0, 1), (1, 0)]
    sd = jax.ShapeDtypeStruct
    scratch = [pltpu.VMEM((n * rows, HD), F32)]
    half = HALF * HD
    pair_shape = sd((2, half, tok), BF16)
    q, k, v, g = (
        jnp.swapaxes(a, 2, 3).reshape(2 * half, tok)
        for a in (queries, key_proj, value_proj, attn_grad)
    )

    z_size = lax.axis_size("z")
    ahead = [(z, z + 1) for z in range(z_size - 1)]
    even_up = [(2 * i, 2 * j) for i, j in ahead]
    even_down = [(2 * j, 2 * i) for i, j in ahead]
    odd_up = [(2 * i + 1, 2 * j + 1) for i, j in ahead]
    odd_down = [(2 * j + 1, 2 * i + 1) for i, j in ahead]
    cols, ch = conv_grad.shape[2:]
    tiles = ch // (2 * LANES)
    cuts = [tiles * part // 22 for part in CUTS] + [tiles]
    starts = [LANES * c for c in cuts[:-1]]
    widths = [LANES * (d - c) for c, d in zip(cuts, cuts[1:])]
    token = sd((8, LANES), F32)

    def hold(i, count):
        return [pltpu.VMEM((cols, widths[i]), BF16)] * count

    def hold_weight(i):
        return [pltpu.VMEM((3, 3, widths[i]), F32)]

    def sems(count):
        return [pltpu.SemaphoreType.DMA((count,))]

    def halve(i, after):
        return call(
            functools.partial(halve_body, starts[i]),
            [sd((cols, widths[i]), BF16)] * 2 + [sd((3, 3, widths[i]), F32), token],
            (held_in_hbm(conv_grad), held_in_hbm(conv_weight)),
            sems(3),
            after=after,
            any_in=True,
        )

    def move_in(i):
        near = lax.ppermute(row_send[i], "x", swap)
        return held_in_hbm(near), held_in_hbm(lax.ppermute(row_mine[i], ("z", "x"), even_down + odd_up))

    def send_out(i):
        return call(
            send_body,
            [sd((cols, widths[i]), BF16), token],
            (row_mine[i], near[i], far[i], weight[i]),
            hold(i, 3) + hold_weight(i) + hold(i, 1) + [pltpu.SemaphoreType.DMA((PIECES, 5))],
            flops=SEND_COST,
            any_in=True,
            hbm_out=1,
        )

    def finish(i, before=()):
        return call(
            keep_body,
            [sd(conv_grad.shape, BF16), token],
            (row_mine[i], near[i], onward[i], back[i], weight[i], *before),
            hold(i, 3) + hold_weight(i) + hold(i, 2) + [pltpu.SemaphoreType.DMA((PIECES, 7))],
            flops=KEEP_COST,
            any_in=True,
            hbm_out=1,
            alias={5: 0} if before else None,
        )

    row_mine, row_send, weight, halved, near, far = {}, {}, {}, {}, {}, {}
    sent, onward, back, kept = {}, {}, {}, {}
    for i in range(CHUNKS):
        row_send[i], row_mine[i], weight[i], halved[i] = call(
            first_body,
            [sd((cols, widths[i]), BF16)] * 2 + [sd((3, 3, widths[i]), F32), token],
            tuple(map(held_in_hbm, (conv_grad, conv_weight))),
            sems(3),
            any_in=True,
        )
        near[i], far[i] = move_in(i)
        onward[i] = lax.ppermute(near[i], ("z", "x"), even_up + odd_down)
        out_send, sent[i] = send_out(i)
        back[i] = lax.ppermute(out_send, "x", swap)
        input_grad, kept[i] = finish(i, (input_grad,) if i else ())
    def part(first, second, after=()):
        return call(
            send_half,
            [pair_shape] * 2,
            (held_in_hbm(first), held_in_hbm(second)),
            sems(4),
            after=after,
            any_in=True,
        )

    kv_send, kv = part(k, v)
    kv_got = lax.ppermute(kv_send, "c", swap)
    qg_send, qg = part(q, g)
    qg_got = lax.ppermute(qg_send, "c", swap)

    def exchange(pay):
        return lax.all_to_all(pay, CHIPS, split_axis=0, concat_axis=0, tiled=True)

    macs = HALF * 2 * tok * HD * HD
    pay, started = call(
        functools.partial(state_body, n, rows),
        [sd((n, pay_one, HD), F32), token],
        (kv, kv_got),
        scratch,
        flops=2 * macs,
        after=(halved[0],),
        pinned=1,
    )
    got = exchange(pay)
    ties = {"near": near, "far": far, "sent": sent, "kept": kept}

    def tied(stage):
        return tuple(ties[name][i] for name, i in ORDER[stage])

    pay, norm, inv = call(
        functools.partial(grad_body, n, rows, scale),
        [sd((n, pay_two, HD), F32), sd((HALF, HD), F32), sd((HALF, 2 * tok), F32)],
        (got, qg, qg_got),
        scratch,
        flops=4 * macs,
        pinned=1,
        after=tied(0),
    )
    got = exchange(pay)
    pay, query_mine, query_send = call(
        functools.partial(query_body, n, rows, scale),
        [sd((n, pay_one, HD), F32)] + [sd((half, tok), BF16)] * 2,
        (got, qg, qg_got, norm, inv),
        scratch,
        flops=4 * macs,
        pinned=1,
        after=tied(1),
    )
    query_got = lax.ppermute(query_send, "c", swap)
    whole_shape = sd((2 * half, tok), BF16)
    query_out, merged = call(merge_query, [whole_shape, token], (query_mine, query_got))
    got = exchange(pay)
    key_mine, key_send = call(
        functools.partial(key_body, n, rows),
        [pair_shape] * 2,
        (got, kv, kv_got),
        scratch,
        flops=8 * macs,
        after=(merged, *tied(2)),
    )
    key_got = lax.ppermute(key_send, "c", swap)
    own = call(place_own, [whole_shape] * 2, (key_mine,), sems(2), any_in=True, hbm_out=2)
    outs = query_out, *call(
        place_far,
        [whole_shape] * 2,
        (key_got, *own),
        sems(2),
        any_in=True,
        hbm_out=2,
        alias={1: 0, 2: 1},
    )
    outs = [jnp.swapaxes(o.reshape(*queries.shape[:2], 2 * half, -1), 2, 3) for o in outs]
    return (*outs, input_grad)


def solution(mesh):
    frames, bands = mesh.shape["frame"], mesh.shape["row"]
    fine = Mesh(mesh.devices.reshape(frames // 2, 2, bands // 2, 2), ("y", "c", "z", "x"))
    split = P(("y", "c"), ("z", "x"), None, None)
    return jax.shard_map(
        shards,
        mesh=fine,
        in_specs=(split,) * 5 + (P(),),
        out_specs=(split,) * 4,
        check_vma=False,
    )
```

```python
import functools
import math

import jax
import jax.numpy as jnp
from jax import lax
from jax.experimental import pallas as pl
from jax.experimental.pallas import tpu as pltpu
from jax.sharding import Mesh, PartitionSpec as P

HEADS = 10
HD = 112
EPSILON = 1e-06
HALF = HEADS // 2
LANES = 128
PIECES = 4
CUTS = (0,)
CHUNKS = 1
EARLY = 1
ORDER = [[], [('sent', 0)], [('kept', 0)]]
SEND_COST = 500000000
KEEP_COST = 10000000000
CHIPS = ("z", "x", "y")
F32 = jnp.float32
BF16 = jnp.bfloat16

NT = (((1,), (1,)), ((), ()))
TN = (((0,), (0,)), ((), ()))
NN = (((1,), (0,)), ((), ()))


def held_in_hbm(x):
    return pltpu.with_memory_space_constraint(x, pltpu.HBM)


def call(body, outs, args, scratch=(), flops=0, after=(), any_in=False, hbm_out=0, pinned=0, alias=None):
    size = sum(math.prod(a.shape) * a.dtype.itemsize for a in list(args) + list(outs))
    fast = pl.BlockSpec(memory_space=pltpu.VMEM)
    slow = pl.BlockSpec(memory_space=pltpu.HBM)
    free = pl.BlockSpec(memory_space=pl.ANY)
    scratch = list(scratch)
    if pinned:
        scratch += [pltpu.VMEM(o.shape, o.dtype) for o in outs[:pinned]]
        scratch += [pltpu.SemaphoreType.DMA((pinned,))]

    def ordered(*refs):
        ins = refs[: len(args)]
        made = refs[len(args) + len(after) :][: len(outs)]
        held = refs[len(args) + len(after) + len(outs) :]
        if not pinned:
            body(*ins, *made, *held)
            return
        *held, sem = held
        kept, held = held[-pinned:], held[:-pinned]
        body(*ins, *kept, *made[pinned:], *held)
        copy_all(list(zip(kept, made)), sem)

    out_specs = [slow if i < max(hbm_out, pinned) else fast for i in range(len(outs))]
    shapes = [
        pltpu.HBM(o.shape, o.dtype) if i < max(hbm_out, pinned) else o
        for i, o in enumerate(outs)
    ]
    return pl.pallas_call(
        ordered,
        out_shape=shapes,
        in_specs=[free if any_in else fast] * len(args) + [free] * len(after),
        out_specs=out_specs,
        scratch_shapes=scratch,
        compiler_params=pltpu.CompilerParams(vmem_limit_bytes=16 * 1024 * 1024),
        cost_estimate=pl.CostEstimate(flops=flops, bytes_accessed=size, transcendentals=0),
        input_output_aliases=alias or {},
    )(*args, *after)


def copy_all(pairs, sems):
    copies = [pltpu.make_async_copy(a, b, sems.at[i]) for i, (a, b) in enumerate(pairs)]
    for c in copies:
        c.start()
    for c in copies:
        c.wait()


def dot(a, b, dims):
    return lax.dot_general(a, b, dims, preferred_element_type=F32)


def pieces(x):
    hi = x.astype(BF16)
    lo = (x - hi.astype(F32)).astype(BF16)
    return hi, lo


def pieces3(x):
    hi = x.astype(BF16)
    mid, lo = pieces(x - hi.astype(F32))
    return [hi, mid, lo]


def exact_rows(row, mat, dims):
    stack = jnp.concatenate(pieces3(row), axis=0)
    return jnp.sum(dot(stack, mat, dims), axis=0, keepdims=True)


def send_half(a_ref, b_ref, send_ref, own_ref, sems):
    mine, theirs = halves(send_ref.shape[1])
    pairs = [
        (a_ref.at[theirs], send_ref.at[0]),
        (b_ref.at[theirs], send_ref.at[1]),
        (a_ref.at[mine], own_ref.at[0]),
        (b_ref.at[mine], own_ref.at[1]),
    ]
    copy_all(pairs, sems)


def first_body(row, weight, send, mine, weight_mine, token, sems):
    token[...] = jnp.zeros(token.shape, F32)
    side = lax.axis_index("x")
    half = mine.shape[1]
    own = columns_at(side * half, half)
    other = columns_at((1 - side) * half, half)
    pairs = [
        (row.at[0, 0, :, own], mine),
        (row.at[0, 0, :, other], send),
        (weight.at[:, :, own], weight_mine),
    ]
    copy_all(pairs, sems)


def halves(size):
    core = lax.axis_index("c")
    mine = pl.ds(pl.multiple_of(core * size, 16), size)
    theirs = pl.ds(pl.multiple_of((1 - core) * size, 16), size)
    return mine, theirs


def merge_query(own, far, out, token):
    token[...] = jnp.zeros(token.shape, F32)
    mine, theirs = halves(own.shape[0])
    out[mine] = own[...]
    out[theirs] = far[...]


def place_own(own, first, second, sems):
    mine, _ = halves(own.shape[1])
    copy_all([(own.at[0], first.at[mine]), (own.at[1], second.at[mine])], sems)


def place_far(far, first_in, second_in, first, second, sems):
    _, theirs = halves(far.shape[1])
    copy_all([(far.at[0], first.at[theirs]), (far.at[1], second.at[theirs])], sems)


def head_of(own, got, i, h):
    part = slice(h * HD, (h + 1) * HD)
    return jnp.concatenate([own[i, part], got[i, part]], axis=1)


def columns(rows):
    wide = jnp.concatenate([rows, jnp.zeros((HALF, LANES - HD), F32)], axis=1)
    tall = jnp.concatenate([wide, jnp.zeros((8 - HALF, LANES), F32)], axis=0)
    return jnp.transpose(tall)


def spread(row, n):
    return jnp.broadcast_to(row[None], (n, 1, HD))


def sum_of(got, n, first, last):
    total = got[0, first:last]
    for j in range(1, n):
        total = total + got[j, first:last]
    return total


def state_body(n, rows, kv, kv_got, pay, token, whole):
    token[...] = jnp.zeros(token.shape, F32)
    for h in range(HALF):
        key = jnp.maximum(head_of(kv, kv_got, 0, h), 0)
        val = head_of(kv, kv_got, 1, h)
        whole[h * HD : (h + 1) * HD] = dot(key, val, NT)
        norm = dot(jnp.ones((8, key.shape[1]), BF16), key, NT)[:1]
        pay[:, rows + h : rows + h + 1] = spread(norm, n)
    for j in range(n):
        pay[j, :rows] = whole[j * rows : (j + 1) * rows]


def grad_body(n, rows, scale, got, qg, qg_got, pay, norm_ref, inv_ref, whole):
    total = sum_of(got, n, 0, rows + HALF)
    norm_ref[...] = total[rows:]
    for h in range(HALF):
        query = jnp.maximum(head_of(qg, qg_got, 0, h), 0)
        grad = head_of(qg, qg_got, 1, h)
        inv = 1.0 / (exact_rows(total[rows + h : rows + h + 1], query, NN) + EPSILON)
        inv_ref[h : h + 1] = inv
        hi, lo = pieces(grad.astype(F32) * (inv * scale))
        whole[h * HD : (h + 1) * HD] = dot(query, hi, NT) + dot(query, lo, NT)
    shard = total[:rows]
    for j in range(n):
        pay[j, :rows] = shard
        pay[j, rows : 2 * rows] = whole[j * rows : (j + 1) * rows]


def scaled_state(whole, qg, qg_got, inv_ref, scale, h):
    feat = jnp.maximum(head_of(qg, qg_got, 0, h), 0)
    grad = head_of(qg, qg_got, 1, h)
    hi, lo = pieces(whole[h * HD : (h + 1) * HD])
    prod = dot(hi, grad, NN) + dot(lo, grad, NN)
    query = feat.astype(F32)
    inv = inv_ref[h : h + 1]
    weight = inv * scale
    proj = jnp.sum(query * prod, axis=0, keepdims=True) * weight * inv
    return feat, query, prod, weight, proj


def norm_body(n, rows, scale, got, qg, qg_got, inv_ref, pay, whole):
    total = sum_of(got, n, rows, 2 * rows)
    for j in range(n):
        whole[j * rows : (j + 1) * rows] = got[j, :rows]
        pay[j, :rows] = total
    for h in range(HALF):
        feat, _, _, _, proj = scaled_state(whole, qg, qg_got, inv_ref, scale, h)
        pay[:, rows + h : rows + h + 1] = spread(-exact_rows(proj, feat, NT), n)


def query_body(scale, whole, qg, qg_got, norm_ref, inv_ref, out_mine, out_theirs):
    norms = columns(norm_ref[...])
    tok = out_mine.shape[1]
    for h in range(HALF):
        part = slice(h * HD, (h + 1) * HD)
        _, query, prod, weight, proj = scaled_state(whole, qg, qg_got, inv_ref, scale, h)
        out = prod * weight - norms[:HD, h : h + 1] * proj
        out = jnp.where(query > 0, out, 0.0).astype(BF16)
        out_mine[part] = out[:, :tok]
        out_theirs[part] = out[:, tok:]


def key_body(n, rows, got, kv, kv_got, out_mine, out_theirs, whole):
    for j in range(n):
        whole[j * rows : (j + 1) * rows] = got[j, :rows]
    norms = columns(sum_of(got, n, rows, rows + HALF))
    tok = out_mine.shape[2]
    for h in range(HALF):
        part = slice(h * HD, (h + 1) * HD)
        key = head_of(kv, kv_got, 0, h)
        val = head_of(kv, kv_got, 1, h)
        hi, lo = pieces(whole[part])
        k_out = dot(hi, val, NN) + dot(lo, val, NN) + norms[:HD, h : h + 1]
        k_out = jnp.where(key.astype(F32) > 0, k_out, 0.0).astype(BF16)
        feat = jnp.maximum(key, 0)
        v_out = (dot(hi, feat, TN) + dot(lo, feat, TN)).astype(BF16)
        out_mine[0, part] = k_out[:, :tok]
        out_theirs[0, part] = k_out[:, tok:]
        out_mine[1, part] = v_out[:, :tok]
        out_theirs[1, part] = v_out[:, tok:]


def shift(x, step):
    rows = lax.broadcasted_iota(jnp.int32, x.shape, 0)
    moved = pltpu.roll(x, step % x.shape[0], 0)
    edge = 0 if step > 0 else x.shape[0] - 1
    return jnp.where(rows == edge, 0.0, moved)


def taps(sources, weight, picks, lanes):
    planes = [ref[:, lanes].astype(F32) for ref in sources]

    def column(j):
        return sum(p * weight[i, pl.ds(j, 1), lanes] for p, i in zip(planes, picks))

    return (column(1) + shift(column(0), -1) + shift(column(2), 1)).astype(BF16)


def columns_at(start, width):
    return pl.ds(pl.multiple_of(start, LANES), width)


def halve_body(at, row, weight, send, mine, weight_mine, token, sems):
    token[...] = jnp.zeros(token.shape, F32)
    side = lax.axis_index("x")
    half, width = row.shape[3] // 2, mine.shape[1]
    pairs = [
        row.at[0, 0, :, columns_at((1 - side) * half + at, width)],
        row.at[0, 0, :, columns_at(side * half + at, width)],
        weight.at[:, :, columns_at(side * half + at, width)],
    ]
    copy_all(list(zip(pairs, (send, mine, weight_mine))), sems)


def pieces_of(width):
    step = -(-(width // LANES) // PIECES) * LANES
    return [(at, min(step, width - at)) for at in range(0, width, step)]


def staged(sources, held, sems, made, picks, out_of):
    width = made.shape[1]
    loads, stores = [], []
    for n, (at, size) in enumerate(pieces_of(width)):
        part = pl.ds(at, size)
        group = []
        for m, (a, b) in enumerate(zip(sources, held)):
            index = (slice(None),) * (len(a.shape) - 1) + (part,)
            group.append(pltpu.make_async_copy(a.at[index], b.at[index], sems.at[n, m]))
        for c in group:
            c.start()
        loads.append(group)
    *planes, weight = held[:4]
    for n, (at, size) in enumerate(pieces_of(width)):
        for c in loads[n]:
            c.wait()

        @pl.loop(at // LANES, (at + size) // LANES)
        def _(t):
            lanes = columns_at(t * LANES, LANES)
            made[:, lanes] = taps(planes, weight, picks, lanes)

        for m, (a, b) in enumerate(out_of(at, size)):
            c = pltpu.make_async_copy(a, b, sems.at[n, len(sources) + m])
            c.start()
            stores.append(c)
    for c in stores:
        c.wait()


def send_body(mine, got, far, weight, out, token, *held):
    *held, made, sems = held
    token[...] = jnp.zeros(token.shape, F32)
    side = lax.axis_index("x")

    def out_of(at, size):
        return [(made.at[:, pl.ds(at, size)], out.at[:, pl.ds(at, size)])]

    staged((got, mine, far, weight), held, sems, made, (1, 2 - 2 * side, 2 * side), out_of)


def keep_body(mine, got, far, back, weight, out, token, *held):
    *held, made, sems = held
    token[...] = jnp.zeros(token.shape, F32)
    side = lax.axis_index("x")
    half = out.shape[3] // 2

    def out_of(at, size):
        here = columns_at(side * half + at, size)
        there = columns_at((1 - side) * half + at, size)
        part = pl.ds(at, size)
        back_held = held[4]
        return [
            (made.at[:, part], out.at[0, 0, :, here]),
            (back_held.at[:, part], out.at[0, 0, :, there]),
        ]

    sources = (mine, got, far, weight, back)
    staged(sources, held, sems, made, (1, 2 * side, 2 - 2 * side), out_of)


def shards(queries, key_proj, value_proj, attn_grad, conv_grad, conv_weight):
    tok = queries.shape[0] * queries.shape[1] * queries.shape[2]
    tokens_all = tok * lax.axis_size(("y", "c", "z", "x"))
    scale = math.sqrt(tokens_all)
    n = lax.axis_size(CHIPS)
    rows = -(-HALF * HD // n)
    pay_one = -(-(rows + HALF) // 8) * 8
    pay_two = -(-2 * rows // 8) * 8
    swap = [(0, 1), (1, 0)]
    sd = jax.ShapeDtypeStruct
    scratch = [pltpu.VMEM((n * rows, HD), F32)]
    half = HALF * HD
    pair_shape = sd((2, half, tok), BF16)
    q, k, v, g = (
        jnp.swapaxes(a, 2, 3).reshape(2 * half, tok)
        for a in (queries, key_proj, value_proj, attn_grad)
    )

    z_size = lax.axis_size("z")
    ahead = [(z, z + 1) for z in range(z_size - 1)]
    even_up = [(2 * i, 2 * j) for i, j in ahead]
    even_down = [(2 * j, 2 * i) for i, j in ahead]
    odd_up = [(2 * i + 1, 2 * j + 1) for i, j in ahead]
    odd_down = [(2 * j + 1, 2 * i + 1) for i, j in ahead]
    cols, ch = conv_grad.shape[2:]
    tiles = ch // (2 * LANES)
    cuts = [tiles * part // 22 for part in CUTS] + [tiles]
    starts = [LANES * c for c in cuts[:-1]]
    widths = [LANES * (d - c) for c, d in zip(cuts, cuts[1:])]
    token = sd((8, LANES), F32)

    def hold(i, count):
        return [pltpu.VMEM((cols, widths[i]), BF16)] * count

    def hold_weight(i):
        return [pltpu.VMEM((3, 3, widths[i]), F32)]

    def sems(count):
        return [pltpu.SemaphoreType.DMA((count,))]

    def halve(i, after):
        return call(
            functools.partial(halve_body, starts[i]),
            [sd((cols, widths[i]), BF16)] * 2 + [sd((3, 3, widths[i]), F32), token],
            (held_in_hbm(conv_grad), held_in_hbm(conv_weight)),
            sems(3),
            after=after,
            any_in=True,
        )

    def move_in(i):
        near = lax.ppermute(row_send[i], "x", swap)
        return held_in_hbm(near), held_in_hbm(lax.ppermute(row_mine[i], ("z", "x"), even_down + odd_up))

    def send_out(i):
        return call(
            send_body,
            [sd((cols, widths[i]), BF16), token],
            (row_mine[i], near[i], far[i], weight[i]),
            hold(i, 3) + hold_weight(i) + hold(i, 1) + [pltpu.SemaphoreType.DMA((PIECES, 5))],
            flops=SEND_COST,
            any_in=True,
            hbm_out=1,
        )

    def finish(i, before=()):
        return call(
            keep_body,
            [sd(conv_grad.shape, BF16), token],
            (row_mine[i], near[i], onward[i], back[i], weight[i], *before),
            hold(i, 3) + hold_weight(i) + hold(i, 2) + [pltpu.SemaphoreType.DMA((PIECES, 7))],
            flops=KEEP_COST,
            any_in=True,
            hbm_out=1,
            alias={5: 0} if before else None,
        )

    row_mine, row_send, weight, halved, near, far = {}, {}, {}, {}, {}, {}
    sent, onward, back, kept = {}, {}, {}, {}
    for i in range(CHUNKS):
        row_send[i], row_mine[i], weight[i], halved[i] = call(
            first_body,
            [sd((cols, widths[i]), BF16)] * 2 + [sd((3, 3, widths[i]), F32), token],
            tuple(map(held_in_hbm, (conv_grad, conv_weight))),
            sems(3),
            any_in=True,
        )
        near[i], far[i] = move_in(i)
        onward[i] = lax.ppermute(near[i], ("z", "x"), even_up + odd_down)
        out_send, sent[i] = send_out(i)
        back[i] = lax.ppermute(out_send, "x", swap)
        input_grad, kept[i] = finish(i, (input_grad,) if i else ())
    def part(first, second, after=()):
        return call(
            send_half,
            [pair_shape] * 2,
            (held_in_hbm(first), held_in_hbm(second)),
            sems(4),
            after=after,
            any_in=True,
        )

    kv_send, kv = part(k, v)
    kv_got = lax.ppermute(kv_send, "c", swap)
    qg_send, qg = part(q, g)
    qg_got = lax.ppermute(qg_send, "c", swap)

    def exchange(pay):
        return lax.all_to_all(pay, CHIPS, split_axis=0, concat_axis=0, tiled=True)

    macs = HALF * 2 * tok * HD * HD
    pay, started = call(
        functools.partial(state_body, n, rows),
        [sd((n, pay_one, HD), F32), token],
        (kv, kv_got),
        scratch,
        flops=2 * macs,
        after=(halved[0],),
        pinned=1,
    )
    got = exchange(pay)
    ties = {"near": near, "far": far, "sent": sent, "kept": kept}

    def tied(stage):
        return tuple(ties[name][i] for name, i in ORDER[stage])

    pay, norm, inv = call(
        functools.partial(grad_body, n, rows, scale),
        [sd((n, pay_two, HD), F32), sd((HALF, HD), F32), sd((HALF, 2 * tok), F32)],
        (got, qg, qg_got),
        scratch,
        flops=4 * macs,
        pinned=1,
        after=tied(0),
    )
    got = exchange(pay)
    pay, state = call(
        functools.partial(norm_body, n, rows, scale),
        [sd((n, pay_one, HD), F32), sd((n * rows, HD), F32)],
        (got, qg, qg_got, inv),
        flops=4 * macs,
        pinned=1,
        after=tied(1),
    )
    query_mine, query_send = call(
        functools.partial(query_body, scale),
        [sd((half, tok), BF16)] * 2,
        (state, qg, qg_got, norm, inv),
        flops=4 * macs,
    )
    query_got = lax.ppermute(query_send, "c", swap)
    whole_shape = sd((2 * half, tok), BF16)
    query_out, merged = call(merge_query, [whole_shape, token], (query_mine, query_got))
    got = exchange(pay)
    key_mine, key_send = call(
        functools.partial(key_body, n, rows),
        [pair_shape] * 2,
        (got, kv, kv_got),
        scratch,
        flops=8 * macs,
        after=(merged, *tied(2)),
    )
    key_got = lax.ppermute(key_send, "c", swap)
    own = call(place_own, [whole_shape] * 2, (key_mine,), sems(2), any_in=True, hbm_out=2)
    outs = query_out, *call(
        place_far,
        [whole_shape] * 2,
        (key_got, *own),
        sems(2),
        any_in=True,
        hbm_out=2,
        alias={1: 0, 2: 1},
    )
    outs = [jnp.swapaxes(o.reshape(*queries.shape[:2], 2 * half, -1), 2, 3) for o in outs]
    return (*outs, input_grad)


def solution(mesh):
    frames, bands = mesh.shape["frame"], mesh.shape["row"]
    fine = Mesh(mesh.devices.reshape(frames // 2, 2, bands // 2, 2), ("y", "c", "z", "x"))
    split = P(("y", "c"), ("z", "x"), None, None)
    return jax.shard_map(
        shards,
        mesh=fine,
        in_specs=(split,) * 5 + (P(),),
        out_specs=(split,) * 4,
        check_vma=False,
    )
```

```python
import functools
import math

import jax
import jax.numpy as jnp
from jax import lax
from jax.experimental import pallas as pl
from jax.experimental.pallas import tpu as pltpu
from jax.sharding import Mesh, PartitionSpec as P

HEADS = 10
HD = 112
EPSILON = 1e-06
HALF = HEADS // 2
LANES = 128
PIECES = 4
CUTS = (0,)
CHUNKS = 1
EARLY = 1
ORDER = [[], [('sent', 0)], [('kept', 0)]]
SEND_COST = 500000000
KEEP_COST = 10000000000
CHIPS = ("z", "x", "y")
F32 = jnp.float32
BF16 = jnp.bfloat16

NT = (((1,), (1,)), ((), ()))
TN = (((0,), (0,)), ((), ()))
NN = (((1,), (0,)), ((), ()))


def held_in_hbm(x):
    return pltpu.with_memory_space_constraint(x, pltpu.HBM)


def call(body, outs, args, scratch=(), flops=0, after=(), any_in=False, hbm_out=0, pinned=0, alias=None):
    size = sum(math.prod(a.shape) * a.dtype.itemsize for a in list(args) + list(outs))
    fast = pl.BlockSpec(memory_space=pltpu.VMEM)
    slow = pl.BlockSpec(memory_space=pltpu.HBM)
    free = pl.BlockSpec(memory_space=pl.ANY)
    scratch = list(scratch)
    if pinned:
        scratch += [pltpu.VMEM(o.shape, o.dtype) for o in outs[:pinned]]
        scratch += [pltpu.SemaphoreType.DMA((pinned,))]

    def ordered(*refs):
        ins = refs[: len(args)]
        made = refs[len(args) + len(after) :][: len(outs)]
        held = refs[len(args) + len(after) + len(outs) :]
        if not pinned:
            body(*ins, *made, *held)
            return
        *held, sem = held
        kept, held = held[-pinned:], held[:-pinned]
        body(*ins, *kept, *made[pinned:], *held)
        copy_all(list(zip(kept, made)), sem)

    out_specs = [slow if i < max(hbm_out, pinned) else fast for i in range(len(outs))]
    shapes = [
        pltpu.HBM(o.shape, o.dtype) if i < max(hbm_out, pinned) else o
        for i, o in enumerate(outs)
    ]
    return pl.pallas_call(
        ordered,
        out_shape=shapes,
        in_specs=[free if any_in else fast] * len(args) + [free] * len(after),
        out_specs=out_specs,
        scratch_shapes=scratch,
        compiler_params=pltpu.CompilerParams(vmem_limit_bytes=16 * 1024 * 1024),
        cost_estimate=pl.CostEstimate(flops=flops, bytes_accessed=size, transcendentals=0),
        input_output_aliases=alias or {},
    )(*args, *after)


def copy_all(pairs, sems):
    copies = [pltpu.make_async_copy(a, b, sems.at[i]) for i, (a, b) in enumerate(pairs)]
    for c in copies:
        c.start()
    for c in copies:
        c.wait()


def dot(a, b, dims):
    return lax.dot_general(a, b, dims, preferred_element_type=F32)


def pieces(x):
    hi = x.astype(BF16)
    lo = (x - hi.astype(F32)).astype(BF16)
    return hi, lo


def pieces3(x):
    hi = x.astype(BF16)
    mid, lo = pieces(x - hi.astype(F32))
    return [hi, mid, lo]


def exact_rows(row, mat, dims):
    stack = jnp.concatenate(pieces3(row), axis=0)
    return jnp.sum(dot(stack, mat, dims), axis=0, keepdims=True)


def send_half(a_ref, b_ref, send_ref, own_ref, sems):
    mine, theirs = halves(send_ref.shape[1])
    pairs = [
        (a_ref.at[theirs], send_ref.at[0]),
        (b_ref.at[theirs], send_ref.at[1]),
        (a_ref.at[mine], own_ref.at[0]),
        (b_ref.at[mine], own_ref.at[1]),
    ]
    copy_all(pairs, sems)


def first_body(row, weight, send, mine, weight_mine, token, sems):
    token[...] = jnp.zeros(token.shape, F32)
    side = lax.axis_index("x")
    half = mine.shape[1]
    own = columns_at(side * half, half)
    other = columns_at((1 - side) * half, half)
    pairs = [
        (row.at[0, 0, :, own], mine),
        (row.at[0, 0, :, other], send),
        (weight.at[:, :, own], weight_mine),
    ]
    copy_all(pairs, sems)


def halves(size):
    core = lax.axis_index("c")
    mine = pl.ds(pl.multiple_of(core * size, 16), size)
    theirs = pl.ds(pl.multiple_of((1 - core) * size, 16), size)
    return mine, theirs


def merge_query(own, far, out, token):
    token[...] = jnp.zeros(token.shape, F32)
    mine, theirs = halves(own.shape[0])
    out[mine] = own[...]
    out[theirs] = far[...]


def place_own(own, first, second, sems):
    mine, _ = halves(own.shape[1])
    copy_all([(own.at[0], first.at[mine]), (own.at[1], second.at[mine])], sems)


def place_far(far, first_in, second_in, first, second, sems):
    _, theirs = halves(far.shape[1])
    copy_all([(far.at[0], first.at[theirs]), (far.at[1], second.at[theirs])], sems)


def head_of(own, got, i, h):
    part = slice(h * HD, (h + 1) * HD)
    return jnp.concatenate([own[i, part], got[i, part]], axis=1)


def columns(rows):
    wide = jnp.concatenate([rows, jnp.zeros((HALF, LANES - HD), F32)], axis=1)
    tall = jnp.concatenate([wide, jnp.zeros((8 - HALF, LANES), F32)], axis=0)
    return jnp.transpose(tall)


def spread(row, n):
    return jnp.broadcast_to(row[None], (n, 1, HD))


def sum_of(got, n, first, last):
    total = got[0, first:last]
    for j in range(1, n):
        total = total + got[j, first:last]
    return total


def deliver(pay, out, whole, sems, n, rows, first, done, todo):
    while todo and (todo[0] + 1) * rows <= done or todo and done >= HALF * HD:
        j = todo.pop(0)
        pay[j, first : first + rows] = whole[j * rows : (j + 1) * rows]
        pltpu.make_async_copy(pay.at[j], out.at[j], sems.at[j]).start()


def arrive(pay, out, sems, n):
    for j in range(n):
        pltpu.make_async_copy(pay.at[j], out.at[j], sems.at[j]).wait()


def state_body(n, rows, kv, kv_got, out, token, whole, pay, sems):
    token[...] = jnp.zeros(token.shape, F32)
    for h in range(HALF):
        key = jnp.maximum(head_of(kv, kv_got, 0, h), 0)
        norm = dot(jnp.ones((8, key.shape[1]), BF16), key, NT)[:1]
        pay[:, rows + h : rows + h + 1] = spread(norm, n)
    todo = list(range(n))
    for h in range(HALF):
        key = jnp.maximum(head_of(kv, kv_got, 0, h), 0)
        val = head_of(kv, kv_got, 1, h)
        whole[h * HD : (h + 1) * HD] = dot(key, val, NT)
        deliver(pay, out, whole, sems, n, rows, 0, (h + 1) * HD, todo)
    arrive(pay, out, sems, n)


def grad_body(n, rows, scale, got, qg, qg_got, out, norm_ref, inv_ref, whole, pay, sems):
    total = sum_of(got, n, 0, rows + HALF)
    norm_ref[...] = total[rows:]
    shard = total[:rows]
    for j in range(n):
        pay[j, :rows] = shard
    todo = list(range(n))
    for h in range(HALF):
        query = jnp.maximum(head_of(qg, qg_got, 0, h), 0)
        grad = head_of(qg, qg_got, 1, h)
        inv = 1.0 / (exact_rows(total[rows + h : rows + h + 1], query, NN) + EPSILON)
        inv_ref[h : h + 1] = inv
        hi, lo = pieces(grad.astype(F32) * (inv * scale))
        whole[h * HD : (h + 1) * HD] = dot(query, hi, NT) + dot(query, lo, NT)
        deliver(pay, out, whole, sems, n, rows, rows, (h + 1) * HD, todo)
    arrive(pay, out, sems, n)


def scaled_state(whole, qg, qg_got, inv_ref, scale, h):
    feat = jnp.maximum(head_of(qg, qg_got, 0, h), 0)
    grad = head_of(qg, qg_got, 1, h)
    hi, lo = pieces(whole[h * HD : (h + 1) * HD])
    prod = dot(hi, grad, NN) + dot(lo, grad, NN)
    query = feat.astype(F32)
    inv = inv_ref[h : h + 1]
    weight = inv * scale
    proj = jnp.sum(query * prod, axis=0, keepdims=True) * weight * inv
    return feat, query, prod, weight, proj


def norm_body(n, rows, scale, got, qg, qg_got, inv_ref, pay, whole):
    total = sum_of(got, n, rows, 2 * rows)
    for j in range(n):
        whole[j * rows : (j + 1) * rows] = got[j, :rows]
        pay[j, :rows] = total
    for h in range(HALF):
        feat, _, _, _, proj = scaled_state(whole, qg, qg_got, inv_ref, scale, h)
        pay[:, rows + h : rows + h + 1] = spread(-exact_rows(proj, feat, NT), n)


def query_body(scale, whole, qg, qg_got, norm_ref, inv_ref, out_mine, out_theirs):
    norms = columns(norm_ref[...])
    tok = out_mine.shape[1]
    for h in range(HALF):
        part = slice(h * HD, (h + 1) * HD)
        _, query, prod, weight, proj = scaled_state(whole, qg, qg_got, inv_ref, scale, h)
        out = prod * weight - norms[:HD, h : h + 1] * proj
        out = jnp.where(query > 0, out, 0.0).astype(BF16)
        out_mine[part] = out[:, :tok]
        out_theirs[part] = out[:, tok:]


def key_body(n, rows, got, kv, kv_got, out_mine, out_theirs, whole):
    for j in range(n):
        whole[j * rows : (j + 1) * rows] = got[j, :rows]
    norms = columns(sum_of(got, n, rows, rows + HALF))
    tok = out_mine.shape[2]
    for h in range(HALF):
        part = slice(h * HD, (h + 1) * HD)
        key = head_of(kv, kv_got, 0, h)
        val = head_of(kv, kv_got, 1, h)
        hi, lo = pieces(whole[part])
        k_out = dot(hi, val, NN) + dot(lo, val, NN) + norms[:HD, h : h + 1]
        k_out = jnp.where(key.astype(F32) > 0, k_out, 0.0).astype(BF16)
        feat = jnp.maximum(key, 0)
        v_out = (dot(hi, feat, TN) + dot(lo, feat, TN)).astype(BF16)
        out_mine[0, part] = k_out[:, :tok]
        out_theirs[0, part] = k_out[:, tok:]
        out_mine[1, part] = v_out[:, :tok]
        out_theirs[1, part] = v_out[:, tok:]


def shift(x, step):
    rows = lax.broadcasted_iota(jnp.int32, x.shape, 0)
    moved = pltpu.roll(x, step % x.shape[0], 0)
    edge = 0 if step > 0 else x.shape[0] - 1
    return jnp.where(rows == edge, 0.0, moved)


def taps(sources, weight, picks, lanes):
    planes = [ref[:, lanes].astype(F32) for ref in sources]

    def column(j):
        return sum(p * weight[i, pl.ds(j, 1), lanes] for p, i in zip(planes, picks))

    return (column(1) + shift(column(0), -1) + shift(column(2), 1)).astype(BF16)


def columns_at(start, width):
    return pl.ds(pl.multiple_of(start, LANES), width)


def halve_body(at, row, weight, send, mine, weight_mine, token, sems):
    token[...] = jnp.zeros(token.shape, F32)
    side = lax.axis_index("x")
    half, width = row.shape[3] // 2, mine.shape[1]
    pairs = [
        row.at[0, 0, :, columns_at((1 - side) * half + at, width)],
        row.at[0, 0, :, columns_at(side * half + at, width)],
        weight.at[:, :, columns_at(side * half + at, width)],
    ]
    copy_all(list(zip(pairs, (send, mine, weight_mine))), sems)


def pieces_of(width):
    step = -(-(width // LANES) // PIECES) * LANES
    return [(at, min(step, width - at)) for at in range(0, width, step)]


def staged(sources, held, sems, made, picks, out_of):
    width = made.shape[1]
    loads, stores = [], []
    for n, (at, size) in enumerate(pieces_of(width)):
        part = pl.ds(at, size)
        group = []
        for m, (a, b) in enumerate(zip(sources, held)):
            index = (slice(None),) * (len(a.shape) - 1) + (part,)
            group.append(pltpu.make_async_copy(a.at[index], b.at[index], sems.at[n, m]))
        for c in group:
            c.start()
        loads.append(group)
    *planes, weight = held[:4]
    for n, (at, size) in enumerate(pieces_of(width)):
        for c in loads[n]:
            c.wait()

        @pl.loop(at // LANES, (at + size) // LANES)
        def _(t):
            lanes = columns_at(t * LANES, LANES)
            made[:, lanes] = taps(planes, weight, picks, lanes)

        for m, (a, b) in enumerate(out_of(at, size)):
            c = pltpu.make_async_copy(a, b, sems.at[n, len(sources) + m])
            c.start()
            stores.append(c)
    for c in stores:
        c.wait()


def send_body(mine, got, far, weight, out, token, *held):
    *held, made, sems = held
    token[...] = jnp.zeros(token.shape, F32)
    side = lax.axis_index("x")

    def out_of(at, size):
        return [(made.at[:, pl.ds(at, size)], out.at[:, pl.ds(at, size)])]

    staged((got, mine, far, weight), held, sems, made, (1, 2 - 2 * side, 2 * side), out_of)


def keep_body(mine, got, far, back, weight, out, token, *held):
    *held, made, sems = held
    token[...] = jnp.zeros(token.shape, F32)
    side = lax.axis_index("x")
    half = out.shape[3] // 2

    def out_of(at, size):
        here = columns_at(side * half + at, size)
        there = columns_at((1 - side) * half + at, size)
        part = pl.ds(at, size)
        back_held = held[4]
        return [
            (made.at[:, part], out.at[0, 0, :, here]),
            (back_held.at[:, part], out.at[0, 0, :, there]),
        ]

    sources = (mine, got, far, weight, back)
    staged(sources, held, sems, made, (1, 2 * side, 2 - 2 * side), out_of)


def shards(queries, key_proj, value_proj, attn_grad, conv_grad, conv_weight):
    tok = queries.shape[0] * queries.shape[1] * queries.shape[2]
    tokens_all = tok * lax.axis_size(("y", "c", "z", "x"))
    scale = math.sqrt(tokens_all)
    n = lax.axis_size(CHIPS)
    rows = -(-HALF * HD // n)
    pay_one = -(-(rows + HALF) // 8) * 8
    pay_two = -(-2 * rows // 8) * 8
    swap = [(0, 1), (1, 0)]
    sd = jax.ShapeDtypeStruct
    scratch = [pltpu.VMEM((n * rows, HD), F32)]
    half = HALF * HD
    pair_shape = sd((2, half, tok), BF16)
    q, k, v, g = (
        jnp.swapaxes(a, 2, 3).reshape(2 * half, tok)
        for a in (queries, key_proj, value_proj, attn_grad)
    )

    z_size = lax.axis_size("z")
    ahead = [(z, z + 1) for z in range(z_size - 1)]
    even_up = [(2 * i, 2 * j) for i, j in ahead]
    even_down = [(2 * j, 2 * i) for i, j in ahead]
    odd_up = [(2 * i + 1, 2 * j + 1) for i, j in ahead]
    odd_down = [(2 * j + 1, 2 * i + 1) for i, j in ahead]
    cols, ch = conv_grad.shape[2:]
    tiles = ch // (2 * LANES)
    cuts = [tiles * part // 22 for part in CUTS] + [tiles]
    starts = [LANES * c for c in cuts[:-1]]
    widths = [LANES * (d - c) for c, d in zip(cuts, cuts[1:])]
    token = sd((8, LANES), F32)

    def hold(i, count):
        return [pltpu.VMEM((cols, widths[i]), BF16)] * count

    def hold_weight(i):
        return [pltpu.VMEM((3, 3, widths[i]), F32)]

    def sems(count):
        return [pltpu.SemaphoreType.DMA((count,))]

    def halve(i, after):
        return call(
            functools.partial(halve_body, starts[i]),
            [sd((cols, widths[i]), BF16)] * 2 + [sd((3, 3, widths[i]), F32), token],
            (held_in_hbm(conv_grad), held_in_hbm(conv_weight)),
            sems(3),
            after=after,
            any_in=True,
        )

    def move_in(i):
        near = lax.ppermute(row_send[i], "x", swap)
        return held_in_hbm(near), held_in_hbm(lax.ppermute(row_mine[i], ("z", "x"), even_down + odd_up))

    def send_out(i):
        return call(
            send_body,
            [sd((cols, widths[i]), BF16), token],
            (row_mine[i], near[i], far[i], weight[i]),
            hold(i, 3) + hold_weight(i) + hold(i, 1) + [pltpu.SemaphoreType.DMA((PIECES, 5))],
            flops=SEND_COST,
            any_in=True,
            hbm_out=1,
        )

    def finish(i, before=()):
        return call(
            keep_body,
            [sd(conv_grad.shape, BF16), token],
            (row_mine[i], near[i], onward[i], back[i], weight[i], *before),
            hold(i, 3) + hold_weight(i) + hold(i, 2) + [pltpu.SemaphoreType.DMA((PIECES, 7))],
            flops=KEEP_COST,
            any_in=True,
            hbm_out=1,
            alias={5: 0} if before else None,
        )

    row_mine, row_send, weight, halved, near, far = {}, {}, {}, {}, {}, {}
    sent, onward, back, kept = {}, {}, {}, {}
    for i in range(CHUNKS):
        row_send[i], row_mine[i], weight[i], halved[i] = call(
            first_body,
            [sd((cols, widths[i]), BF16)] * 2 + [sd((3, 3, widths[i]), F32), token],
            tuple(map(held_in_hbm, (conv_grad, conv_weight))),
            sems(3),
            any_in=True,
        )
        near[i], far[i] = move_in(i)
        onward[i] = lax.ppermute(near[i], ("z", "x"), even_up + odd_down)
        out_send, sent[i] = send_out(i)
        back[i] = lax.ppermute(out_send, "x", swap)
        input_grad, kept[i] = finish(i, (input_grad,) if i else ())
    def part(first, second, after=()):
        return call(
            send_half,
            [pair_shape] * 2,
            (held_in_hbm(first), held_in_hbm(second)),
            sems(4),
            after=after,
            any_in=True,
        )

    kv_send, kv = part(k, v)
    kv_got = lax.ppermute(kv_send, "c", swap)
    qg_send, qg = part(q, g)
    qg_got = lax.ppermute(qg_send, "c", swap)

    def exchange(pay):
        return lax.all_to_all(pay, CHIPS, split_axis=0, concat_axis=0, tiled=True)

    macs = HALF * 2 * tok * HD * HD
    pay, started = call(
        functools.partial(state_body, n, rows),
        [sd((n, pay_one, HD), F32), token],
        (kv, kv_got),
        scratch + [pltpu.VMEM((n, pay_one, HD), F32), pltpu.SemaphoreType.DMA((n,))],
        flops=2 * macs,
        after=(halved[0],),
        hbm_out=1,
    )
    got = exchange(pay)
    ties = {"near": near, "far": far, "sent": sent, "kept": kept}

    def tied(stage):
        return tuple(ties[name][i] for name, i in ORDER[stage])

    pay, norm, inv = call(
        functools.partial(grad_body, n, rows, scale),
        [sd((n, pay_two, HD), F32), sd((HALF, HD), F32), sd((HALF, 2 * tok), F32)],
        (got, qg, qg_got),
        scratch + [pltpu.VMEM((n, pay_two, HD), F32), pltpu.SemaphoreType.DMA((n,))],
        flops=4 * macs,
        hbm_out=1,
        after=tied(0),
    )
    got = exchange(pay)
    pay, state = call(
        functools.partial(norm_body, n, rows, scale),
        [sd((n, pay_one, HD), F32), sd((n * rows, HD), F32)],
        (got, qg, qg_got, inv),
        flops=4 * macs,
        pinned=1,
        after=tied(1),
    )
    query_mine, query_send = call(
        functools.partial(query_body, scale),
        [sd((half, tok), BF16)] * 2,
        (state, qg, qg_got, norm, inv),
        flops=4 * macs,
    )
    query_got = lax.ppermute(query_send, "c", swap)
    whole_shape = sd((2 * half, tok), BF16)
    query_out, merged = call(merge_query, [whole_shape, token], (query_mine, query_got))
    got = exchange(pay)
    key_mine, key_send = call(
        functools.partial(key_body, n, rows),
        [pair_shape] * 2,
        (got, kv, kv_got),
        scratch,
        flops=8 * macs,
        after=(merged, *tied(2)),
    )
    key_got = lax.ppermute(key_send, "c", swap)
    own = call(place_own, [whole_shape] * 2, (key_mine,), sems(2), any_in=True, hbm_out=2)
    outs = query_out, *call(
        place_far,
        [whole_shape] * 2,
        (key_got, *own),
        sems(2),
        any_in=True,
        hbm_out=2,
        alias={1: 0, 2: 1},
    )
    outs = [jnp.swapaxes(o.reshape(*queries.shape[:2], 2 * half, -1), 2, 3) for o in outs]
    return (*outs, input_grad)


def solution(mesh):
    frames, bands = mesh.shape["frame"], mesh.shape["row"]
    fine = Mesh(mesh.devices.reshape(frames // 2, 2, bands // 2, 2), ("y", "c", "z", "x"))
    split = P(("y", "c"), ("z", "x"), None, None)
    return jax.shard_map(
        shards,
        mesh=fine,
        in_specs=(split,) * 5 + (P(),),
        out_specs=(split,) * 4,
        check_vma=False,
    )
```
